256 devices in a mesh: dp: 16 (over z, y_lo), blk: 16 (over x, y_hi, core).
Axes of the slice: x: 4, y: 4 (y_hi: 2, y_lo: 2; y = y_hi * 2 + y_lo), z: 8, core: 2. Of those that a mesh axis runs over, the one named last changes fastest.
Arguments:
- image: bfloat16 [65536, 768], P(('dp', 'blk')), may hold values from -100 to 100
- text: bfloat16 [65536, 768], P(('dp', 'blk')), may hold values from -100 to 100
- positive: int32 [65536], P(('dp', 'blk')), may hold values from 0 to 255, as said below
- logit_scale: float32 [1], replicated, may hold values from 10 to 300
Outputs:
- loss: float32 [1], replicated
- scale_grad: float32 [1], replicated
- image_grad: bfloat16 [65536, 768], P(('dp', 'blk'))
- text_grad: bfloat16 [65536, 768], P(('dp', 'blk'))
The draws below stay inside these ranges and needn't reach their ends.
Inputs may be any that keep to these rules, and one draw needn't show every extreme that they name: `positive`: within each aligned block of 256 rows (the rows of one device) the entries are a permutation of 0 to 255.
All inputs are finite; a program needn't handle non-finite values.
Results may differ from the reference program's by a relative error of at most 0.0055.
The reference program's roundings to bfloat16 on the way (of `img_unit`, `txt_unit` and `weight_bf`) count: a program that leaves them out, or rounds other values in their place, can miss the bound.
Values may be sent and summed in bfloat16 or wider, within the bound.
No kernel may reach another device: no remote copies, remote signals or barrier semaphores. Data moves between devices by JAX's collectives and lax.ppermute only.
A program may use at most 64 MiB of HBM per device.

```python
import math
import jax
import jax.numpy as jnp
from jax import lax

D = 768
ROWS = 256
GROUP = 4096
TOTAL = 65536
N_DP = 16


def block_order(block_key):
    return jax.random.permutation(block_key, ROWS).astype(jnp.int32)


def pairing(key):
    block_keys = jax.random.split(key, TOTAL // ROWS)
    orders = jax.vmap(block_order)(block_keys)
    return orders.reshape(TOTAL).astype(jnp.int32)


def mixed_noise(noise_key):
    gauss = jax.random.normal(noise_key, (TOTAL, D), jnp.float32)
    return gauss


def row_spread(spread_key):
    return jnp.exp(jax.random.uniform(spread_key, (TOTAL, 1), jnp.float32, 0.0, math.log(10.0)))


def text_field(key):
    noise_key, spread_key = jax.random.split(jax.random.fold_in(key, 101), 2)
    spread = row_spread(spread_key)
    field = mixed_noise(noise_key) * spread
    return field


def image_field(key, order, field):
    noise_key, spread_key = jax.random.split(key)
    index = jnp.arange(TOTAL, dtype=jnp.int32)
    partner = field[index // ROWS * ROWS + order]
    noise = mixed_noise(noise_key)
    spread = row_spread(spread_key)
    place = (index // ROWS).astype(jnp.float32)
    share = 0.2 + 0.7 * place / max(TOTAL // ROWS - 1, 1)
    result = share[:, None] * partner + jnp.sqrt(1.0 - share * share)[:, None] * noise * spread
    return result


def draw_positive(key, part):
    return pairing(key)


def draw_text(key, part):
    field = text_field(key)
    return jnp.clip(field, -100.0, 100.0).astype(jnp.bfloat16)


def draw_image(key, part):
    order = pairing(key)
    field = text_field(key)
    key = jax.random.fold_in(key, 3)
    values = image_field(key, order, field)
    return jnp.clip(values, -100.0, 100.0).astype(jnp.bfloat16)


def draw_logit_scale(key, part):
    key = jax.random.fold_in(key, 4)
    return jax.random.uniform(key, (1,), jnp.float32, 10.0, 30.0)


def setup_inputs(seed: int = 0) -> dict:
    arg_keys = jax.random.split(jax.random.key(seed), 5)
    return {
        "image": draw_image(jax.random.fold_in(arg_keys[4], 71), 0),
        "text": draw_text(jax.random.fold_in(arg_keys[4], 71), 0),
        "positive": draw_positive(jax.random.fold_in(arg_keys[4], 71), 0),
        "logit_scale": draw_logit_scale(jax.random.fold_in(arg_keys[4], 71), 0),
    }


EPSILON = 1e-06

def unit_rows(values):
    wide = values.astype(jnp.float32)
    inverse = lax.rsqrt(lax.optimization_barrier(jnp.sum(wide * wide, axis=-1, keepdims=True)) + EPSILON)
    direction = wide * inverse
    return (direction, direction.astype(jnp.bfloat16), inverse)

def back_rows(direction, inverse, incoming):
    along = lax.optimization_barrier(jnp.sum(direction * incoming, axis=-1, keepdims=True))
    return ((incoming - direction * along) * inverse).astype(jnp.bfloat16)

def reference(image, text, positive, logit_scale):
    scale = logit_scale[0]
    images = image.reshape(N_DP, GROUP, D)
    texts = text.reshape(N_DP, GROUP, D)
    pairs = positive.reshape(N_DP, GROUP)

    def one_group(items):
        img, txt, pair = items
        img_dir, img_unit, img_inv = unit_rows(img)
        txt_dir, txt_unit, txt_inv = unit_rows(txt)
        logits = scale * jnp.dot(img_unit, txt_unit.T, preferred_element_type=jnp.float32)
        columns = jnp.arange(GROUP, dtype=jnp.int32)
        target = columns // ROWS * ROWS + pair.astype(jnp.int32)
        row_lse = jax.nn.logsumexp(logits, axis=1)
        col_lse = jax.nn.logsumexp(logits, axis=0)
        hit = columns[None, :] == target[:, None]
        matched = lax.optimization_barrier(jnp.sum(jnp.where(hit, logits, jnp.zeros_like(logits)), axis=1))
        loss_part = 0.5 * (jnp.sum(row_lse) + jnp.sum(col_lse)) - jnp.sum(matched)
        weight = 0.5 * (jnp.exp(logits - row_lse[:, None]) + jnp.exp(logits - col_lse[None, :])) - hit.astype(logits.dtype)
        slope = jnp.sum(weight * logits)
        weight_bf = weight.astype(jnp.bfloat16)
        img_back = scale * jnp.dot(weight_bf, txt_unit, preferred_element_type=jnp.float32)
        txt_back = scale * jnp.dot(weight_bf.T, img_unit, preferred_element_type=jnp.float32)
        return (back_rows(img_dir, img_inv, img_back), back_rows(txt_dir, txt_inv, txt_back), loss_part, slope)
    image_grad, text_grad, loss_parts, slopes = lax.map(one_group, (images, texts, pairs))
    loss = (jnp.sum(loss_parts) / TOTAL).reshape(1)
    scale_grad = (jnp.sum(slopes) / (TOTAL * scale)).reshape(1)
    return (loss, scale_grad, image_grad.reshape(TOTAL, D), text_grad.reshape(TOTAL, D))
```

```python
import functools

import jax
import jax.numpy as jnp
from jax import lax
from jax.experimental import pallas as pl
from jax.experimental.pallas import tpu as pltpu
from jax.sharding import PartitionSpec as P

EPSILON = 1e-06
PART = jnp.float32
VMEM = pl.BlockSpec(memory_space=pltpu.VMEM)
SMEM = pl.BlockSpec(memory_space=pltpu.SMEM)
PARAMS = pltpu.CompilerParams(vmem_limit_bytes=40 * 1024 * 1024)
SLOTS = 4


def swapped(value, axis, bits):
    return lax.ppermute(value, axis, [(i, i ^ bits) for i in range(lax.axis_size(axis))])


def eye(n):
    return lax.broadcasted_iota(jnp.int32, (n, n), 0) == lax.broadcasted_iota(jnp.int32, (n, n), 1)


def to_row(column, diagonal):
    return jnp.sum(jnp.where(diagonal, column, 0.0), axis=0, keepdims=True)


def to_column(row, diagonal):
    return jnp.sum(jnp.where(diagonal, row, 0.0), axis=1, keepdims=True)


def unit_rows(values):
    wide = values.astype(jnp.float32)
    inverse = lax.rsqrt(jnp.sum(wide * wide, axis=-1, keepdims=True) + EPSILON)
    return wide * inverse, inverse


def scores(scale, left, right):
    return scale * lax.dot_general(
        left, right, (((1,), (1,)), ((), ())), preferred_element_type=jnp.float32
    )


def unit_kernel(image, text, img_unit, txt_unit):
    img_unit[...] = unit_rows(image[...])[0].astype(jnp.bfloat16)
    txt_unit[...] = unit_rows(text[...])[0].astype(jnp.bfloat16)


def stats_kernel(scale, *refs):
    imgs, txts = refs[:SLOTS], refs[SLOTS : 2 * SLOTS]
    row_part, col_part, logits = refs[2 * SLOTS :]
    rows = imgs[0].shape[0]
    diagonal = eye(rows)
    span = lambda k: pl.ds(k * rows, rows)
    row_top, col_top = [None] * SLOTS, [None] * SLOTS
    for k in range(SLOTS):
        for l in range(SLOTS):
            tile = scores(scale[0], imgs[k][...], txts[l][...])
            logits[span(k), span(l)] = tile
            right = jnp.max(tile, axis=1, keepdims=True)
            down = jnp.max(tile, axis=0, keepdims=True)
            row_top[k] = right if l == 0 else jnp.maximum(row_top[k], right)
            col_top[l] = down if k == 0 else jnp.maximum(col_top[l], down)
    col_sum = [jnp.zeros((1, rows), jnp.float32)] * SLOTS
    for k in range(SLOTS):
        row_sum = jnp.zeros((rows, 1), jnp.float32)
        for l in range(SLOTS):
            tile = logits[span(k), span(l)]
            row_sum += jnp.sum(jnp.exp(tile - row_top[k]), axis=1, keepdims=True)
            col_sum[l] += jnp.sum(jnp.exp(tile - col_top[l]), axis=0, keepdims=True)
        row_part[pl.ds(k, 1), :] = to_row(row_top[k], diagonal) + jnp.log(to_row(row_sum, diagonal))
    for l in range(SLOTS):
        col_part[pl.ds(l, 1), :] = col_top[l] + jnp.log(col_sum[l])


def joined(parts):
    top = functools.reduce(jnp.maximum, parts)
    return top + jnp.log(sum(jnp.exp(part - top) for part in parts))


def back_kernel(scale, *refs):
    imgs, txts = refs[:SLOTS], refs[SLOTS : 2 * SLOTS]
    row_parts, col_parts = refs[2 * SLOTS : 3 * SLOTS], refs[3 * SLOTS : 4 * SLOTS]
    positive = refs[4 * SLOTS]
    outs = refs[4 * SLOTS + 1 :]
    img_back, txt_back, sums = outs[:SLOTS], outs[SLOTS : 2 * SLOTS], outs[2 * SLOTS]
    rows = imgs[0].shape[0]
    diagonal = eye(rows)
    lse = lambda parts, k: joined([parts[m][pl.ds(k ^ m, 1), :] for m in range(SLOTS)])
    row_lse = [lse(row_parts, k) for k in range(SLOTS)]
    col_lse = [lse(col_parts, l) for l in range(SLOTS)]
    target = to_column(positive[...].astype(jnp.float32), diagonal).astype(jnp.int32)
    hit = lax.broadcasted_iota(jnp.int32, (rows, rows), 1) == target
    slope = jnp.zeros((1, 1), jnp.float32)
    txt_sum = [None] * SLOTS
    for k in (1, 2, 3, 0):
        img_sum = None
        right = to_column(row_lse[k], diagonal)
        for l in range(SLOTS):
            tile = scores(scale[0], imgs[k][...], txts[l][...])
            weight = 0.5 * (jnp.exp(tile - right) + jnp.exp(tile - col_lse[l]))
            if k == 0 and l == 0:
                weight = weight - hit.astype(jnp.float32)
                matched = jnp.sum(jnp.where(hit, tile, 0.0), keepdims=True)
            slope += jnp.sum(weight * tile, keepdims=True)
            narrow = weight.astype(jnp.bfloat16)
            img_term = jnp.dot(narrow, txts[l][...], preferred_element_type=jnp.float32)
            txt_term = lax.dot_general(
                narrow, imgs[k][...], (((0,), (0,)), ((), ())), preferred_element_type=jnp.float32
            )
            img_sum = img_term if l == 0 else img_sum + img_term
            if k == 1:
                txt_back_acc = txt_term
            else:
                txt_back_acc = txt_sum[l][...] + txt_term
            if k == 0:
                txt_back[l][...] = txt_back_acc.astype(txt_back[l].dtype)
            else:
                refs[-1][l] = txt_back_acc
                txt_sum[l] = refs[-1].at[l]
        img_back[k][...] = img_sum.astype(img_back[k].dtype)
    loss = 0.5 * (
        jnp.sum(row_lse[0], keepdims=True) + jnp.sum(col_lse[0], keepdims=True)
    ) - matched
    lane = lax.broadcasted_iota(jnp.int32, sums.shape, 1)
    sums[...] = jnp.where(lane == 0, loss, jnp.where(lane == 1, slope, 0.0))


def grad_kernel(scale, image, text, *refs):
    img_parts, txt_parts = refs[:SLOTS], refs[SLOTS : 2 * SLOTS]
    for values, parts, out in zip((image, text), (img_parts, txt_parts), refs[2 * SLOTS :]):
        direction, inverse = unit_rows(values[...])
        incoming = scale[0] * sum(part[...].astype(jnp.float32) for part in parts)
        along = jnp.sum(direction * incoming, axis=-1, keepdims=True)
        out[...] = ((incoming - direction * along) * inverse).astype(out.dtype)


def shards(image, text, positive, logit_scale):
    rows, width = image.shape
    shape = jax.ShapeDtypeStruct
    block = shape((rows, width), jnp.bfloat16)
    img_unit, txt_unit = pl.pallas_call(
        unit_kernel, out_shape=[block] * 2, in_specs=[VMEM] * 2, out_specs=[VMEM] * 2,
        compiler_params=PARAMS, name="unit",
    )(image, text)
    along_x = [m << 2 for m in range(SLOTS)]
    along_y = list(range(SLOTS))
    spread = lambda value, bits: [value] + [swapped(value, "blk", b) for b in bits[1:]]
    imgs = spread(img_unit, along_x)
    txts = spread(txt_unit, along_y)
    part = shape((SLOTS, rows), jnp.float32)
    row_part, col_part = pl.pallas_call(
        stats_kernel, out_shape=[part] * 2,
        in_specs=[SMEM] + [VMEM] * (2 * SLOTS), out_specs=[VMEM] * 2,
        scratch_shapes=[pltpu.VMEM((SLOTS * rows, SLOTS * rows), jnp.float32)],
        compiler_params=PARAMS, name="stats",
    )(logit_scale, *imgs, *txts)
    row_parts = spread(row_part, along_x)
    col_parts = spread(col_part, along_y)
    wide = shape((rows, width), jnp.float32)
    sent = shape((rows, width), PART)
    outs = pl.pallas_call(
        back_kernel,
        out_shape=([wide] + [sent] * (SLOTS - 1)) * 2 + [shape((8, 128), jnp.float32)],
        in_specs=[SMEM] + [VMEM] * (4 * SLOTS + 1), out_specs=[VMEM] * (2 * SLOTS + 1),
        scratch_shapes=[pltpu.VMEM((SLOTS, rows, width), jnp.float32)],
        compiler_params=PARAMS, name="back",
    )(logit_scale, *imgs, *txts, *row_parts, *col_parts, positive.reshape(1, rows))
    img_back, txt_back, sums = outs[:SLOTS], outs[SLOTS : 2 * SLOTS], outs[2 * SLOTS]
    collect = lambda parts, bits: [parts[0]] + [
        swapped(p, "blk", b) for p, b in zip(parts[1:], bits[1:])
    ]
    img_parts = collect(img_back, along_x)
    txt_parts = collect(txt_back, along_y)
    for axis in ("blk", "dp"):
        step = 1
        while step < lax.axis_size(axis):
            sums = sums + swapped(sums, axis, step)
            step *= 2
    image_grad, text_grad = pl.pallas_call(
        grad_kernel, out_shape=[block] * 2,
        in_specs=[SMEM] + [VMEM] * (2 + 2 * SLOTS), out_specs=[VMEM] * 2,
        compiler_params=PARAMS, name="grad",
    )(logit_scale, image, text, *img_parts, *txt_parts)
    total_rows = rows * lax.axis_size("blk") * lax.axis_size("dp")
    loss = sums[0, :1] / total_rows
    scale_grad = sums[0, 1:2] / (total_rows * logit_scale)
    return (loss, scale_grad, image_grad, text_grad)


def solution(mesh):
    in_specs = (P(("dp", "blk"), None), P(("dp", "blk"), None), P(("dp", "blk")), P())
    out_specs = (P(), P(), P(("dp", "blk"), None), P(("dp", "blk"), None))
    return jax.shard_map(shards, mesh=mesh, in_specs=in_specs, out_specs=out_specs, check_vma=False)
```

```python
import jax
import jax.numpy as jnp
from jax import lax
from jax.experimental import pallas as pl
from jax.experimental.pallas import tpu as pltpu
from jax.sharding import PartitionSpec as P

EPSILON = 1e-06
VMEM = pl.BlockSpec(memory_space=pltpu.VMEM)
SMEM = pl.BlockSpec(memory_space=pltpu.SMEM)
SLOTS = 4
LOW = -1e30
NEAR = (0, 1, 3)
X1, X2, X3, Y, CORE = 4, 8, 12, 2, 1


def swapped(value, bits, axis="blk"):
    return lax.ppermute(value, axis, [(i, i ^ bits) for i in range(lax.axis_size(axis))])


def call(kernel, name, outs, *args, scalar=False):
    specs = [SMEM] * scalar + [VMEM] * (len(args) - scalar)
    return pl.pallas_call(
        kernel, out_shape=[jax.ShapeDtypeStruct(s, d) for s, d in outs], in_specs=specs,
        out_specs=[VMEM] * len(outs), name=name,
        compiler_params=pltpu.CompilerParams(vmem_limit_bytes=24 * 1024 * 1024),
    )(*args)


def eye(n):
    return lax.broadcasted_iota(jnp.int32, (n, n), 0) == lax.broadcasted_iota(jnp.int32, (n, n), 1)


def to_row(column, diagonal):
    return jnp.sum(jnp.where(diagonal, column, 0.0), axis=0, keepdims=True)


def to_column(row, diagonal):
    return jnp.sum(jnp.where(diagonal, row, 0.0), axis=1, keepdims=True)


def unit_rows(values):
    wide = values.astype(jnp.float32)
    inverse = lax.rsqrt(jnp.sum(wide * wide, axis=-1, keepdims=True) + EPSILON)
    return wide * inverse, inverse


def hits(positive, diagonal):
    target = to_column(positive[...].astype(jnp.float32), diagonal).astype(jnp.int32)
    return lax.broadcasted_iota(jnp.int32, diagonal.shape, 1) == target


def merged(a, b):
    top = jnp.maximum(a[0], b[0])
    ea, eb = jnp.exp(a[0] - top), jnp.exp(b[0] - top)
    both = ea + eb
    return top + jnp.log(both), (a[1] * ea + b[1] * eb) / both


def into(part, span, value):
    part[0:1, span], part[1:2, span] = merged((part[0:1, span], part[1:2, span]), value)


def stats(scale, imgs, txts, logits, row_part, col_part):
    diagonal = eye(next(iter(txts.values())).shape[0])
    rows = diagonal.shape[0]
    slots, blocks = tuple(imgs), tuple(txts)
    at = lambda k: pl.ds(k * rows, rows)
    row_top, col_top = {}, {}
    for l in blocks:
        for k in slots:
            tile = scale * lax.dot_general(
                imgs[k][...], txts[l][...], (((1,), (1,)), ((), ())),
                preferred_element_type=jnp.float32,
            )
            logits[k, l][...] = tile
            right = jnp.max(tile, axis=1, keepdims=True)
            down = jnp.max(tile, axis=0, keepdims=True)
            row_top[k] = jnp.maximum(row_top[k], right) if k in row_top else right
            col_top[l] = jnp.maximum(col_top[l], down) if l in col_top else down
    none = jnp.zeros((1, rows), jnp.float32)
    col_sum, col_moment = {l: none for l in blocks}, {l: none for l in blocks}
    for k in slots:
        total = jnp.zeros((rows, 1), jnp.float32)
        moment = jnp.zeros((rows, 1), jnp.float32)
        for l in blocks:
            tile = logits[k, l][...]
            e = jnp.exp(tile - row_top[k])
            total += jnp.sum(e, axis=1, keepdims=True)
            moment += jnp.sum(e * tile, axis=1, keepdims=True)
            f = jnp.exp(tile - col_top[l])
            col_sum[l] += jnp.sum(f, axis=0, keepdims=True)
            col_moment[l] += jnp.sum(f * tile, axis=0, keepdims=True)
        total = to_row(total, diagonal)
        top = to_row(row_top[k], diagonal)
        into(row_part, at(k), (top + jnp.log(total), to_row(moment, diagonal) / total))
    for l in blocks:
        into(col_part, at(l), (col_top[l] + jnp.log(col_sum[l]), col_moment[l] / col_sum[l]))


def unit(values):
    return unit_rows(values[...])[0].astype(jnp.bfloat16)


def views(ref, slots, rows):
    return {k: ref.at[pl.ds(n * rows, rows), :] for n, k in enumerate(slots)}


def tiles(ref, slots, blocks, rows):
    return {
        (k, l): ref.at[pl.ds(n * rows, rows), pl.ds(m * rows, rows)]
        for n, k in enumerate(slots) for m, l in enumerate(blocks)
    }


def first_kernel(
    scale, i0, i1, i3, t0, t1, t2, positive, near, txts, logits, row_part, col_part
):
    rows = i0.shape[0]
    imgs, texts = views(near, NEAR, rows), views(txts, (0, 1, 2), rows)
    for k, raw in ((0, i0), (1, i1), (3, i3)):
        imgs[k][...] = unit(raw)
    for l, raw in ((0, t0), (1, t1), (2, t2)):
        texts[l][...] = unit(raw)
    for part in (row_part, col_part):
        part[0:1, :] = jnp.full((1, SLOTS * rows), LOW, jnp.float32)
        part[1:4, :] = jnp.zeros((3, SLOTS * rows), jnp.float32)
    scores = tiles(logits, NEAR, (0, 1, 2), rows)
    stats(scale[0], imgs, texts, scores, row_part, col_part)
    matched = jnp.where(hits(positive, eye(rows)), scores[0, 0][...], 0.0)
    row_part[2:3, pl.ds(0, rows)] = jnp.sum(matched, axis=0, keepdims=True)


def split_kernel(i1, i3, via1, via3):
    half = via1.shape[0]
    via1[...] = i3[pl.ds(0, half), :]
    via3[...] = i1[pl.ds(half, half), :]


def second_kernel(scale, t3, near, txts_in, row_in, col_in, txts, logits, row_part, col_part):
    rows = t3.shape[0]
    row_part[...] = row_in[...]
    col_part[...] = col_in[...]
    txts[pl.ds(0, 3 * rows), :] = txts_in[...]
    last = txts.at[pl.ds(3 * rows, rows), :]
    last[...] = unit(t3)
    scores = tiles(logits, NEAR, (3,), rows)
    stats(scale[0], views(near, NEAR, rows), {3: last}, scores, row_part, col_part)


def third_kernel(scale, i2a, i2b, txts, row_in, col_in, far, logits, row_part, col_part):
    half = i2a.shape[0]
    rows = 2 * half
    row_part[...] = row_in[...]
    col_part[...] = col_in[...]
    far[pl.ds(0, half), :] = unit(i2a)
    far[pl.ds(half, half), :] = unit(i2b)
    blocks = range(SLOTS)
    scores = tiles(logits, (2,), blocks, rows)
    stats(scale[0], {2: far}, views(txts, blocks, rows), scores, row_part, col_part)


def joined(mine, theirs, bit):
    rows = mine.shape[1] // SLOTS
    swap = lambda at: jnp.concatenate(
        [theirs[at : at + 1, (k ^ bit) * rows : ((k ^ bit) + 1) * rows] for k in range(SLOTS)], axis=1
    )
    value, mean = merged((mine[0:1, :], mine[1:2, :]), (swap(0), swap(1)))
    return value, mean, mine[2:3, :] + swap(2)


def join_kernel(row_a, row_b, col_a, col_b, row, col):
    for a, b, out in ((row_a, row_b, row), (col_a, col_b, col)):
        out[0:1, :], out[1:2, :], out[2:3, :] = joined(a, b, 1)
        out[3:4, :] = jnp.zeros((1, out.shape[1]), jnp.float32)


def lse_kernel(row_a, row_b, col_a, col_b, lse, row_sums, col_sums):
    lane = lax.broadcasted_iota(jnp.int32, row_sums.shape, 1)
    for at, (a, b, out) in enumerate(((row_a, row_b, row_sums), (col_a, col_b, col_sums))):
        value, mean, matched = joined(a, b, 2)
        lse[at : at + 1, :] = value
        add = lambda v: jnp.sum(v, axis=1, keepdims=True)
        loss, slope = add(0.5 * value - matched), add(0.5 * mean - matched)
        out[...] = jnp.where(lane == 0, loss, jnp.where(lane == 1, slope, 0.0))


def over(near_w, far_w, near, far, span):
    term = lambda weights, blocks: lax.dot_general(
        weights[:, span], blocks[...], (((0,), (0,)), ((), ())), preferred_element_type=jnp.float32
    )
    return term(near_w, near) + term(far_w, far)


def weight_kernel(first, second, third, lse, positive, near, far, near_w, far_w, core_part):
    rows = far.shape[0]
    diagonal = eye(rows)
    at = lambda k: pl.ds(k * rows, rows)
    blocks = range(SLOTS)
    scores = tiles(first, NEAR, (0, 1, 2), rows)
    scores.update(tiles(second, NEAR, (3,), rows))
    scores.update(tiles(third, (2,), blocks, rows))
    w = tiles(near_w, NEAR, blocks, rows)
    w.update(tiles(far_w, (2,), blocks, rows))
    for k in range(SLOTS):
        right = to_column(lse[0:1, at(k)], diagonal)
        for l in blocks:
            tile = scores[k, l][...]
            weight = 0.5 * (jnp.exp(tile - right) + jnp.exp(tile - lse[1:2, at(l)]))
            if k == 0 and l == 0:
                weight = weight - hits(positive, diagonal).astype(jnp.float32)
            w[k, l][...] = weight.astype(jnp.bfloat16)
    for n, l in enumerate((1, 3)):
        core_part[at(n), :] = over(near_w, far_w, near, far, at(l)).astype(core_part.dtype)


def home_kernel(
    near_w, far_w, near, far, txts, row_a, row_b, col_a, col_b,
    img_back, txt_back, txt_next, row, col,
):
    rows = img_back.shape[0]
    img_back[...] = jnp.dot(near_w[pl.ds(0, rows), :], txts[...], preferred_element_type=jnp.float32)
    for out, l in ((txt_back, 0), (txt_next, 2)):
        out[...] = over(near_w, far_w, near, far, pl.ds(l * rows, rows))
    row[...] = row_a[...] + row_b[...]
    col[...] = col_a[...] + col_b[...]


def away_kernel(
    near_w, far_w, txts, txt_next, core_part, row_a, row_b, col_a, col_b,
    part1, part2, part3, part_y, sums,
):
    rows = part1.shape[0]
    w = views(near_w, NEAR, rows)
    w[2] = far_w
    for k, out in ((1, part1), (2, part2), (3, part3)):
        back = jnp.dot(w[k][...], txts[...], preferred_element_type=jnp.float32)
        out[...] = back.astype(out.dtype)
    total = txt_next[...] + core_part[pl.ds(rows, rows), :].astype(jnp.float32)
    part_y[...] = total.astype(part_y.dtype)
    sums[...] = (row_a[...] + row_b[...]) + (col_a[...] + col_b[...])


def grad_kernel(scale, image, text, img_back, txt_back, core_part, p1, p2, p3, py, image_grad, text_grad):
    for values, parts, out in (
        (image, (img_back, p1, p2, p3), image_grad), (text, (txt_back, core_part, py), text_grad),
    ):
        direction, inverse = unit_rows(values[...])
        incoming = scale[0] * sum(
            part[pl.ds(0, direction.shape[0]), :].astype(jnp.float32) for part in parts
        )
        along = jnp.sum(direction * incoming, axis=-1, keepdims=True)
        out[...] = ((incoming - direction * along) * inverse).astype(out.dtype)


def shards(image, text, positive, logit_scale):
    rows, width = image.shape
    group = SLOTS * rows
    f32, bf16 = jnp.float32, jnp.bfloat16
    block, parts = ((rows, width), bf16), ((SLOTS, group), f32)
    positive = positive.reshape(1, rows)

    i1, i3 = swapped(image, X1), swapped(image, X3)
    t1, t2 = swapped(text, CORE), swapped(text, Y)
    half = ((rows // 2, width), bf16)
    via1, via3 = call(split_kernel, "split", [half] * 2, i1, i3)
    i2a, i2b = swapped(via1, X1), swapped(via3, X3)
    t3 = swapped(t2, CORE)
    three = group - rows
    near, txts, first, row_part, col_part = call(
        first_kernel, "first", [((three, width), bf16)] * 2 + [((three, three), f32), parts, parts],
        logit_scale, image, i1, i3, text, t1, t2, positive, scalar=True,
    )
    txts, second, row_part, col_part = call(
        second_kernel, "second", [((group, width), bf16), ((three, rows), f32), parts, parts],
        logit_scale, t3, near, txts, row_part, col_part, scalar=True,
    )
    far, third, row_part, col_part = call(
        third_kernel, "third", [block, ((rows, group), f32), parts, parts],
        logit_scale, i2a, i2b, txts, row_part, col_part, scalar=True,
    )
    row_half, col_half = call(
        join_kernel, "join", [parts] * 2,
        row_part, swapped(row_part, X1), col_part, swapped(col_part, CORE),
    )
    lse, row_sums, col_sums = call(
        lse_kernel, "lse", [((2, group), f32)] + [((8, 128), f32)] * 2,
        row_half, swapped(row_half, X2), col_half, swapped(col_half, Y),
    )
    near_w, far_w, core_part = call(
        weight_kernel, "weight",
        [((three, group), bf16), ((rows, group), bf16), ((2 * rows, width), bf16)],
        first, second, third, lse, positive, near, far,
    )
    core_part = swapped(core_part, CORE)
    wide, few = ((rows, width), f32), ((8, 128), f32)
    img_back, txt_back, txt_next, row_sums, col_sums = call(
        home_kernel, "home", [wide] * 3 + [few] * 2, near_w, far_w, near, far, txts,
        row_sums, swapped(row_sums, CORE), col_sums, swapped(col_sums, X1),
    )
    part1, part2, part3, part_y, sums = call(
        away_kernel, "away", [block] * 4 + [few], near_w, far_w, txts, txt_next, core_part,
        row_sums, swapped(row_sums, Y), col_sums, swapped(col_sums, X2),
    )
    part1, part2, part3 = swapped(part1, X1), swapped(part2, X2), swapped(part3, X3)
    part_y = swapped(part_y, Y)
    step = lax.axis_size("dp") // 2
    while step >= 1:
        sums = sums + swapped(sums, step, "dp")
        step //= 2
    image_grad, text_grad = call(
        grad_kernel, "grad", [block] * 2,
        logit_scale, image, text, img_back, txt_back, core_part, part1, part2, part3, part_y, scalar=True,
    )
    total_rows = rows * lax.axis_size("blk") * lax.axis_size("dp")
    loss = sums[0, :1] / total_rows
    scale_grad = sums[0, 1:2] / (total_rows * logit_scale)
    return (loss, scale_grad, image_grad, text_grad)


def solution(mesh):
    in_specs = (P(("dp", "blk"), None), P(("dp", "blk"), None), P(("dp", "blk")), P())
    out_specs = (P(), P(), P(("dp", "blk"), None), P(("dp", "blk"), None))
    return jax.shard_map(shards, mesh=mesh, in_specs=in_specs, out_specs=out_specs, check_vma=False)
```

```python
import functools
import itertools
import math

import jax
import jax.numpy as jnp
from jax import lax
from jax.experimental import pallas as pl
from jax.experimental.pallas import tpu as pltpu
from jax.sharding import PartitionSpec as P

EPSILON = 1e-06
VMEM = pl.BlockSpec(memory_space=pltpu.VMEM)
SMEM = pl.BlockSpec(memory_space=pltpu.SMEM)
PARAMS = pltpu.CompilerParams(vmem_limit_bytes=24 * 1024 * 1024)
SLOTS = 4
LOW = -1e30
COST = {
    "pick": 5.0,
    "own": 0.25, "first": 2.4, "second": 1.05, "third": 1.15, "lse": 0.15, "weight": 1.3,
    "image": 1.1, "text": 1.1, "early": 1.4, "away": 0.3, "grad": 1.6,
}
NEAR = (0, 1, 3)
X1, X2, X3, Y, CORE = 4, 8, 12, 2, 1


def swapped(value, bits, axis="blk"):
    return lax.ppermute(value, axis, [(i, i ^ bits) for i in range(lax.axis_size(axis))])


def moved(value, step):
    places = itertools.product(range(8), range(2), range(4), range(2), range(2))
    flat = lambda z, lo, x, hi, core: (z % 8 * 2 + lo) * 16 + x * 4 + hi * 2 + core
    pairs = [(flat(*p), flat(*step(*p))) for p in places]
    return lax.ppermute(value, ("dp", "blk"), pairs)


def by_sides(z, lo, x, hi, core):
    return (z, 1 - lo, x, 1 - hi, core) if core == 0 else (z, lo, 3 - x, hi, core)


def relay(z, lo, x, hi, core):
    return (z, lo, x ^ 1 if core == 0 else 3 - x, hi, core)


def by_planes(z, lo, x, hi, core):
    return (z + (1 if (z + core) % 2 == 0 else -1), lo, x, hi, core)


def by_far_planes(z, lo, x, hi, core):
    return (z + (-3 if core == 0 else 3), lo, x, hi, core)


def call(kernel, name, outs, *args, scalar=False):
    specs = [SMEM] * scalar + [VMEM] * (len(args) - scalar)
    moved = sum(a.size * a.dtype.itemsize for a in args)
    moved += sum(math.prod(s) * jnp.dtype(d).itemsize for s, d in outs)
    return pl.pallas_call(
        kernel, out_shape=[jax.ShapeDtypeStruct(s, d) for s, d in outs], in_specs=specs,
        out_specs=[VMEM] * len(outs), name=name,
        cost_estimate=pl.CostEstimate(
            flops=int(COST.get(name, 0.05) * 1.1e9), bytes_accessed=moved, transcendentals=0
        ),
        compiler_params=PARAMS,
    )(*args)


def eye(n):
    return lax.broadcasted_iota(jnp.int32, (n, n), 0) == lax.broadcasted_iota(jnp.int32, (n, n), 1)


def to_row(column, diagonal):
    return jnp.sum(jnp.where(diagonal, column, 0.0), axis=0, keepdims=True)


def to_column(row, diagonal):
    return jnp.sum(jnp.where(diagonal, row, 0.0), axis=1, keepdims=True)


def unit_rows(values):
    wide = values.astype(jnp.float32)
    inverse = lax.rsqrt(jnp.sum(wide * wide, axis=-1, keepdims=True) + EPSILON)
    return wide * inverse, inverse


def hits(positive, diagonal):
    target = to_column(positive[...].astype(jnp.float32), diagonal).astype(jnp.int32)
    return lax.broadcasted_iota(jnp.int32, diagonal.shape, 1) == target


def merged(a, b):
    top = jnp.maximum(a[0], b[0])
    ea, eb = jnp.exp(a[0] - top), jnp.exp(b[0] - top)
    both = ea + eb
    return top + jnp.log(both), (a[1] * ea + b[1] * eb) / both


def into(part, span, value):
    part[0:1, span], part[1:2, span] = merged((part[0:1, span], part[1:2, span]), value)


def stats(scale, imgs, txts, logits, row_part, col_part):
    diagonal = eye(next(iter(txts.values())).shape[0])
    rows = diagonal.shape[0]
    slots, blocks = tuple(imgs), tuple(txts)
    at = lambda k: pl.ds(k * rows, rows)
    row_top, col_top = {}, {}
    for l in blocks:
        for k in slots:
            tile = scale * lax.dot_general(
                imgs[k][...], txts[l][...], (((1,), (1,)), ((), ())),
                preferred_element_type=jnp.float32,
            )
            logits[k, l][...] = tile
            right = jnp.max(tile, axis=1, keepdims=True)
            down = jnp.max(tile, axis=0, keepdims=True)
            row_top[k] = jnp.maximum(row_top[k], right) if k in row_top else right
            col_top[l] = jnp.maximum(col_top[l], down) if l in col_top else down
    none = jnp.zeros((1, rows), jnp.float32)
    col_sum, col_moment = {l: none for l in blocks}, {l: none for l in blocks}
    for k in slots:
        total = jnp.zeros((rows, 1), jnp.float32)
        moment = jnp.zeros((rows, 1), jnp.float32)
        for l in blocks:
            tile = logits[k, l][...]
            e = jnp.exp(tile - row_top[k])
            total += jnp.sum(e, axis=1, keepdims=True)
            moment += jnp.sum(e * tile, axis=1, keepdims=True)
            f = jnp.exp(tile - col_top[l])
            col_sum[l] += jnp.sum(f, axis=0, keepdims=True)
            col_moment[l] += jnp.sum(f * tile, axis=0, keepdims=True)
        total = to_row(total, diagonal)
        top = to_row(row_top[k], diagonal)
        into(row_part, at(k), (top + jnp.log(total), to_row(moment, diagonal) / total))
    for l in blocks:
        into(col_part, at(l), (col_top[l] + jnp.log(col_sum[l]), col_moment[l] / col_sum[l]))


def unit(values):
    return unit_rows(values[...])[0].astype(jnp.bfloat16)


def views(ref, slots, rows):
    return {k: ref.at[pl.ds(n * rows, rows), :] for n, k in enumerate(slots)}


def tiles(ref, slots, blocks, rows):
    return {
        (k, l): ref.at[pl.ds(n * rows, rows), pl.ds(m * rows, rows)]
        for n, k in enumerate(slots) for m, l in enumerate(blocks)
    }


def own_kernel(image, text, img_unit, txt_unit):
    img_unit[...] = unit(image)
    txt_unit[...] = unit(text)


def first_kernel(
    scale, i0, t0, i1, i3, t1, t2, positive, near, txts, logits, row_part, col_part
):
    rows = i0.shape[0]
    imgs, texts = views(near, NEAR, rows), views(txts, (0, 1, 2), rows)
    imgs[0][...] = i0[...]
    texts[0][...] = t0[...]
    imgs[1][...], imgs[3][...] = unit(i1), unit(i3)
    texts[1][...], texts[2][...] = unit(t1), unit(t2)
    for part in (row_part, col_part):
        part[0:1, :] = jnp.full((1, SLOTS * rows), LOW, jnp.float32)
        part[1:4, :] = jnp.zeros((3, SLOTS * rows), jnp.float32)
    scores = tiles(logits, NEAR, (0, 1, 2), rows)
    stats(scale[0], imgs, texts, scores, row_part, col_part)
    matched = jnp.where(hits(positive, eye(rows)), scores[0, 0][...], 0.0)
    row_part[2:3, pl.ds(0, rows)] = jnp.sum(matched, axis=0, keepdims=True)


def core_index():
    return lax.axis_index("blk") % 2


def pick_kernel(i1, i3, before, out):
    core = core_index()

    @pl.when(core == 0)
    def _():
        out[...] = i3[...]

    @pl.when(core != 0)
    def _():
        out[...] = i1[...]


def second_kernel(scale, t3, near, txts_in, row_in, col_in, txts, logits, row_part, col_part):
    rows = t3.shape[0]
    row_part[...] = row_in[...]
    col_part[...] = col_in[...]
    txts[pl.ds(0, 3 * rows), :] = txts_in[...]
    last = txts.at[pl.ds(3 * rows, rows), :]
    last[...] = unit(t3)
    scores = tiles(logits, NEAR, (3,), rows)
    stats(scale[0], views(near, NEAR, rows), {3: last}, scores, row_part, col_part)


def third_kernel(scale, i2, txts, row_in, col_in, far, logits, row_part, col_part):
    rows = i2.shape[0]
    row_part[...] = row_in[...]
    col_part[...] = col_in[...]
    far[...] = unit(i2)
    blocks = range(SLOTS)
    scores = tiles(logits, (2,), blocks, rows)
    stats(scale[0], {2: far}, views(txts, blocks, rows), scores, row_part, col_part)


def joined(mine, other, bits):
    rows = mine.shape[1] // SLOTS
    swap = lambda at: jnp.concatenate(
        [other[at : at + 1, (k ^ bits) * rows : ((k ^ bits) + 1) * rows] for k in range(SLOTS)],
        axis=1,
    )
    value, mean = merged((mine[0:1, :], mine[1:2, :]), (swap(0), swap(1)))
    return value, mean, mine[2:3, :] + swap(2)


def join_kernel(mine, other, before, out):
    out[0:1, :], out[1:2, :], out[2:3, :] = joined(mine, other, 1)
    out[3:4, :] = jnp.zeros((1, out.shape[1]), jnp.float32)


def slot_sum(v):
    rows = v.shape[1] // SLOTS
    at = [jnp.sum(v[:, k * rows : (k + 1) * rows], axis=1, keepdims=True) for k in range(SLOTS)]
    return (at[0] + at[1]) + (at[2] + at[3])


def lse_kernel(row, row3, col, col2, lse, row_sums, col_sums):
    lane = lax.broadcasted_iota(jnp.int32, row_sums.shape, 1)
    sides = ((joined(row, row3, 3), row_sums), (joined(col, col2, 2), col_sums))
    for at, ((value, mean, matched), out) in enumerate(sides):
        lse[at : at + 1, :] = value
        loss, slope = slot_sum(0.5 * value - matched), slot_sum(0.5 * mean - matched)
        out[...] = jnp.where(lane == 0, loss, jnp.where(lane == 1, slope, 0.0))


def weigh(scores, lse, slots, w, hit=None):
    rows = lse.shape[1] // SLOTS
    diagonal = eye(rows)
    at = lambda k: pl.ds(k * rows, rows)
    for k in slots:
        right = to_column(lse[0:1, at(k)], diagonal)
        for l in range(SLOTS):
            tile = scores[k, l][...]
            weight = 0.5 * (jnp.exp(tile - right) + jnp.exp(tile - lse[1:2, at(l)]))
            if k == 0 and l == 0:
                weight = weight - hit.astype(jnp.float32)
            w[k, l][...] = weight.astype(jnp.bfloat16)


def over(w01, w23, near, far, l):
    rows = far.shape[0]
    span = pl.ds(l * rows, rows)
    term = lambda weights, blocks: lax.dot_general(
        weights, blocks, (((0,), (0,)), ((), ())), preferred_element_type=jnp.float32
    )
    one, two = pl.ds(0, rows), pl.ds(rows, rows)
    return (
        term(w01[:, span], near[pl.ds(0, 2 * rows), :])
        + term(w23[one, span], far[...])
        + term(w23[two, span], near[pl.ds(2 * rows, rows), :])
    )


def weight_kernel(first, second, third, lse, positive, w01, w23):
    rows = w01.shape[0] // 2
    scores = tiles(first, NEAR, (0, 1, 2), rows)
    scores.update(tiles(second, NEAR, (3,), rows))
    scores.update(tiles(third, (2,), range(SLOTS), rows))
    hit = hits(positive, eye(rows))
    weigh(scores, lse, (2, 3), tiles(w23, (2, 3), range(SLOTS), rows))
    weigh(scores, lse, (0, 1), tiles(w01, (0, 1), range(SLOTS), rows), hit)


def early_kernel(w01, w23, near, far, txts, before, core_part, part2):
    rows = far.shape[0]
    back = jnp.dot(w23[pl.ds(0, rows), :], txts[...], preferred_element_type=jnp.float32)
    part2[...] = back.astype(part2.dtype)
    for n, l in enumerate((1, 3)):
        core_part[pl.ds(n * rows, rows), :] = over(w01, w23, near, far, l).astype(core_part.dtype)


def image_kernel(w01, w23, txts, img_back, part1, part3, token):
    rows = img_back.shape[0]
    token[...] = jnp.zeros(token.shape, jnp.float32)
    for w, n, out in ((w01, 1, part1), (w23, 1, part3), (w01, 0, img_back)):
        out[...] = jnp.dot(w[pl.ds(n * rows, rows), :], txts[...], preferred_element_type=jnp.float32)


def text_kernel(w01, w23, near, far, before, txt_back, txt_next, token):
    token[...] = jnp.zeros(token.shape, jnp.float32)
    for out, l in ((txt_back, 0), (txt_next, 2)):
        out[...] = over(w01, w23, near, far, l)


def away_kernel(wide1, wide3, txt_next, relayed, core_part, before, part1, part3, part_y):
    rows = part1.shape[0]
    passed = relayed[...].astype(jnp.float32)
    zero = core_index() == 0
    part3[...] = (wide3[...] + jnp.where(zero, passed, 0.0)).astype(part3.dtype)
    part1[...] = (wide1[...] + jnp.where(zero, 0.0, passed)).astype(part1.dtype)
    total = txt_next[...] + core_part[pl.ds(rows, rows), :].astype(jnp.float32)
    part_y[...] = total.astype(part_y.dtype)


def half_kernel(row, row_core, col, col1, before, out):
    out[...] = jnp.where(core_index() == 0, row[...] + row_core[...], col[...] + col1[...])


def side_kernel(a, b, before, out):
    out[...] = a[...] + b[...]


def add_kernel(a, b, out):
    out[...] = a[...] + b[...]


def lane_from_z(shape):
    lane = lax.broadcasted_iota(jnp.int32, shape, 1)
    return (lane - lax.axis_index("dp") // 2 + 8) % 8, lane < 8


def total_kernel(mine, other, held):
    sums = mine[0:1, :] + other[0:1, :]
    line = lax.broadcasted_iota(jnp.int32, held.shape, 0)
    value = jnp.where(line == 0, sums[:, 0:1], jnp.where(line == 1, sums[:, 1:2], 0.0))
    ahead, inside = lane_from_z(held.shape)
    held[...] = jnp.where(inside & (ahead == 0), value, 0.0)


def union(held, other, both):
    ahead, _ = lane_from_z(held.shape)
    twice = functools.reduce(jnp.logical_or, [ahead == n for n in both])
    return jnp.where(twice, held[...], held[...] + other[...])


def planes_kernel(held, other, out):
    out[...] = union(held, other, (0,))


def scalar_kernel(total_rows, scale, held, other, before, loss, scale_grad):
    sums = jnp.sum(union(held, other, (0, 1, 4, 7)), axis=1, keepdims=True)
    loss[0] = sums[0, 0] / total_rows
    scale_grad[0] = sums[1, 0] / (total_rows * scale[0])


def grad_kernel(scale, image, text, img_back, txt_back, core_part, p1, p3, py, image_grad, text_grad, token):
    token[...] = jnp.zeros(token.shape, jnp.float32)
    for values, parts, out in (
        (image, (img_back, p1, p3), image_grad), (text, (txt_back, core_part, py), text_grad),
    ):
        direction, inverse = unit_rows(values[...])
        incoming = scale[0] * sum(
            part[pl.ds(0, direction.shape[0]), :].astype(jnp.float32) for part in parts
        )
        along = jnp.sum(direction * incoming, axis=-1, keepdims=True)
        out[...] = ((incoming - direction * along) * inverse).astype(out.dtype)


def shards(image, text, positive, logit_scale):
    rows, width = image.shape
    group = SLOTS * rows
    f32, bf16 = jnp.float32, jnp.bfloat16
    block, parts = ((rows, width), bf16), ((SLOTS, group), f32)
    positive = positive.reshape(1, rows)

    i1, i3 = swapped(image, X1), swapped(image, X3)
    t1, t2 = swapped(text, CORE), swapped(text, Y)
    own_img, own_txt = call(own_kernel, "own", [block] * 2, image, text)
    (on,) = call(pick_kernel, "pick", [block], i1, i3, own_img)
    i2 = moved(on, relay)
    t3 = swapped(t2, CORE)
    three = group - rows
    near, txts, first, row_part, col_part = call(
        first_kernel, "first", [((three, width), bf16)] * 2 + [((three, three), f32), parts, parts],
        logit_scale, own_img, own_txt, i1, i3, t1, t2, positive, scalar=True,
    )
    txts, second, row_part, col_part = call(
        second_kernel, "second", [((group, width), bf16), ((three, rows), f32), parts, parts],
        logit_scale, t3, near, txts, row_part, col_part, scalar=True,
    )
    few = ((8, 128), f32)
    far, third, row_part, col_part = call(
        third_kernel, "third", [block, ((rows, group), f32), parts, parts],
        logit_scale, i2, txts, row_part, col_part, scalar=True,
    )
    (col_part,) = call(join_kernel, "join", [parts], col_part, swapped(col_part, CORE), col_part)
    col_y = swapped(col_part, Y)
    (row_part,) = call(join_kernel, "join", [parts], row_part, swapped(row_part, X1), col_y)
    lse, row_sums, col_sums = call(
        lse_kernel, "lse", [((2, group), f32), few, few],
        row_part, swapped(row_part, X3), col_part, col_y,
    )
    row_core, col1 = swapped(row_sums, CORE), swapped(col_sums, X1)
    heavy = ((2 * rows, group), bf16)
    w01, w23 = call(
        weight_kernel, "weight", [heavy, heavy], first, second, third, lse, positive
    )
    wide = ((rows, width), f32)
    img_back, part1, part3, token = call(image_kernel, "image", [wide] * 3 + [few], w01, w23, txts)
    (sums,) = call(half_kernel, "half", [few], row_sums, row_core, col_sums, col1, token)
    core_part, part2 = call(
        early_kernel, "early", [((2 * rows, width), bf16), block], w01, w23, near, far, txts, sums
    )
    core_part, relayed = swapped(core_part, CORE), moved(part2, relay)
    txt_back, txt_next, token = call(
        text_kernel, "text", [wide] * 2 + [few], w01, w23, near, far, sums
    )
    (sums,) = call(side_kernel, "side", [few], sums, swapped(sums, 1, "dp"), token)
    (sums,) = call(add_kernel, "add", [few], sums, moved(sums, by_sides))
    (held,) = call(total_kernel, "total", [few], sums, swapped(sums, CORE))
    part1, part3, part_y = call(
        away_kernel, "away", [block] * 3, part1, part3, txt_next, relayed, core_part, held
    )
    part1, part3, part_y = swapped(part1, X1), swapped(part3, X3), swapped(part_y, Y)
    (held,) = call(add_kernel, "add", [few], held, moved(held, by_planes))
    (held,) = call(planes_kernel, "planes", [few], held, swapped(held, CORE))
    (held,) = call(add_kernel, "add", [few], held, moved(held, by_far_planes))
    image_grad, text_grad, token = call(
        grad_kernel, "grad", [block] * 2 + [few],
        logit_scale, image, text, img_back, txt_back, core_part, part1, part3, part_y, scalar=True,
    )
    total_rows = rows * lax.axis_size("blk") * lax.axis_size("dp")
    loss, scale_grad = pl.pallas_call(
        functools.partial(scalar_kernel, total_rows), name="scalar",
        out_shape=[jax.ShapeDtypeStruct((1,), f32)] * 2,
        in_specs=[SMEM, VMEM, VMEM, VMEM], out_specs=[SMEM] * 2,
        compiler_params=PARAMS,
    )(logit_scale, held, swapped(held, CORE), token)
    return (loss, scale_grad, image_grad, text_grad)


def solution(mesh):
    in_specs = (P(("dp", "blk"), None), P(("dp", "blk"), None), P(("dp", "blk")), P())
    out_specs = (P(), P(), P(("dp", "blk"), None), P(("dp", "blk"), None))
    return jax.shard_map(shards, mesh=mesh, in_specs=in_specs, out_specs=out_specs, check_vma=False)
```

```python
import functools
import itertools
import math

import jax
import jax.numpy as jnp
from jax import lax
from jax.experimental import pallas as pl
from jax.experimental.pallas import tpu as pltpu
from jax.sharding import PartitionSpec as P

EPSILON = 1e-06
VMEM = pl.BlockSpec(memory_space=pltpu.VMEM)
SMEM = pl.BlockSpec(memory_space=pltpu.SMEM)
PARAMS = pltpu.CompilerParams(vmem_limit_bytes=24 * 1024 * 1024)
SLOTS = 4
LOW = -1e30
COST = {
    "total": 30,
    "pick": 5.0,
    "own": 0.25, "first": 12, "second": 8, "third": 1.15, "lse": 0.15, "weight": 1.3,
    "image": 1.1, "text": 1.1, "early": 1.4, "half": 0.3, "across": 0.2, "late": 0.2, "grad": 1.6,
}
NEAR = (0, 1, 3)
X1, X2, X3, Y, CORE = 4, 8, 12, 2, 1


def swapped(value, bits, axis="blk"):
    return lax.ppermute(value, axis, [(i, i ^ bits) for i in range(lax.axis_size(axis))])


def moved(value, step):
    places = itertools.product(range(8), range(2), range(4), range(2), range(2))
    flat = lambda z, lo, x, hi, core: (z % 8 * 2 + lo) * 16 + x * 4 + hi * 2 + core
    pairs = [(flat(*p), flat(*step(*p))) for p in places]
    return lax.ppermute(value, ("dp", "blk"), pairs)


def by_sides(z, lo, x, hi, core):
    return (z, 1 - lo, x, 1 - hi, core) if core == 0 else (z, lo, 3 - x, hi, core)


def relay(z, lo, x, hi, core):
    return (z, lo, x ^ 1 if core == 0 else 3 - x, hi, core)


def other_way(z, lo, x, hi, core):
    return (z, lo, 3 - x if core == 0 else x ^ 1, hi, core)


def by_planes(z, lo, x, hi, core):
    return (z + (1 if (z + core) % 2 == 0 else -1), lo, x, hi, core)


def by_far_planes(z, lo, x, hi, core):
    return (z + (-3 if core == 0 else 3), lo, x, hi, core)


def call(kernel, name, outs, *args, scalar=False):
    specs = [SMEM] * scalar + [VMEM] * (len(args) - scalar)
    moved = sum(a.size * a.dtype.itemsize for a in args)
    moved += sum(math.prod(s) * jnp.dtype(d).itemsize for s, d in outs)
    return pl.pallas_call(
        kernel, out_shape=[jax.ShapeDtypeStruct(s, d) for s, d in outs], in_specs=specs,
        out_specs=[VMEM] * len(outs), name=name,
        cost_estimate=pl.CostEstimate(
            flops=int(COST.get(name, 0.05) * 1.1e9), bytes_accessed=moved, transcendentals=0
        ),
        compiler_params=PARAMS,
    )(*args)


def eye(n):
    return lax.broadcasted_iota(jnp.int32, (n, n), 0) == lax.broadcasted_iota(jnp.int32, (n, n), 1)


def to_row(column, diagonal):
    return jnp.sum(jnp.where(diagonal, column, 0.0), axis=0, keepdims=True)


def to_column(row, diagonal):
    return jnp.sum(jnp.where(diagonal, row, 0.0), axis=1, keepdims=True)


def unit_rows(values):
    wide = values.astype(jnp.float32)
    inverse = lax.rsqrt(jnp.sum(wide * wide, axis=-1, keepdims=True) + EPSILON)
    return wide * inverse, inverse


def hits(positive, diagonal):
    target = to_column(positive[...].astype(jnp.float32), diagonal).astype(jnp.int32)
    return lax.broadcasted_iota(jnp.int32, diagonal.shape, 1) == target


def merged(a, b):
    top = jnp.maximum(a[0], b[0])
    ea, eb = jnp.exp(a[0] - top), jnp.exp(b[0] - top)
    both = ea + eb
    return top + jnp.log(both), (a[1] * ea + b[1] * eb) / both


def into(part, span, value):
    part[0:1, span], part[1:2, span] = merged((part[0:1, span], part[1:2, span]), value)


def stats(scale, imgs, txts, logits, row_part, col_part):
    diagonal = eye(next(iter(txts.values())).shape[0])
    rows = diagonal.shape[0]
    slots, blocks = tuple(imgs), tuple(txts)
    at = lambda k: pl.ds(k * rows, rows)
    row_top, col_top = {}, {}
    for l in blocks:
        for k in slots:
            tile = scale * lax.dot_general(
                imgs[k][...], txts[l][...], (((1,), (1,)), ((), ())),
                preferred_element_type=jnp.float32,
            )
            logits[k, l][...] = tile
            right = jnp.max(tile, axis=1, keepdims=True)
            down = jnp.max(tile, axis=0, keepdims=True)
            row_top[k] = jnp.maximum(row_top[k], right) if k in row_top else right
            col_top[l] = jnp.maximum(col_top[l], down) if l in col_top else down
    none = jnp.zeros((1, rows), jnp.float32)
    col_sum, col_moment = {l: none for l in blocks}, {l: none for l in blocks}
    for k in slots:
        total = jnp.zeros((rows, 1), jnp.float32)
        moment = jnp.zeros((rows, 1), jnp.float32)
        for l in blocks:
            tile = logits[k, l][...]
            e = jnp.exp(tile - row_top[k])
            total += jnp.sum(e, axis=1, keepdims=True)
            moment += jnp.sum(e * tile, axis=1, keepdims=True)
            f = jnp.exp(tile - col_top[l])
            col_sum[l] += jnp.sum(f, axis=0, keepdims=True)
            col_moment[l] += jnp.sum(f * tile, axis=0, keepdims=True)
        total = to_row(total, diagonal)
        top = to_row(row_top[k], diagonal)
        into(row_part, at(k), (top + jnp.log(total), to_row(moment, diagonal) / total))
    for l in blocks:
        into(col_part, at(l), (col_top[l] + jnp.log(col_sum[l]), col_moment[l] / col_sum[l]))


def unit(values):
    return unit_rows(values[...])[0].astype(jnp.bfloat16)


def views(ref, slots, rows):
    return {k: ref.at[pl.ds(n * rows, rows), :] for n, k in enumerate(slots)}


def tiles(ref, slots, blocks, rows):
    return {
        (k, l): ref.at[pl.ds(n * rows, rows), pl.ds(m * rows, rows)]
        for n, k in enumerate(slots) for m, l in enumerate(blocks)
    }


def own_kernel(image, text, img_unit, txt_unit):
    img_unit[...] = unit(image)
    txt_unit[...] = unit(text)


def first_kernel(
    scale, i0, t0, i1, i3, t1, t2, positive, near, txts, logits, row_part, col_part
):
    rows = i0.shape[0]
    imgs, texts = views(near, NEAR, rows), views(txts, (0, 1, 2), rows)
    imgs[0][...] = i0[...]
    texts[0][...] = t0[...]
    imgs[1][...], imgs[3][...] = unit(i1), unit(i3)
    texts[1][...], texts[2][...] = unit(t1), unit(t2)
    for part in (row_part, col_part):
        part[0:1, :] = jnp.full((1, SLOTS * rows), LOW, jnp.float32)
        part[1:4, :] = jnp.zeros((3, SLOTS * rows), jnp.float32)
    scores = tiles(logits, NEAR, (0, 1, 2), rows)
    stats(scale[0], imgs, texts, scores, row_part, col_part)
    matched = jnp.where(hits(positive, eye(rows)), scores[0, 0][...], 0.0)
    row_part[2:3, pl.ds(0, rows)] = jnp.sum(matched, axis=0, keepdims=True)


def core_index():
    return lax.axis_index("blk") % 2


def pick_kernel(i1, i3, before, out):
    core = core_index()

    @pl.when(core == 0)
    def _():
        out[...] = i3[...]

    @pl.when(core != 0)
    def _():
        out[...] = i1[...]


def second_kernel(scale, t3, near, txts_in, row_in, col_in, txts, logits, row_part, col_part):
    rows = t3.shape[0]
    row_part[...] = row_in[...]
    col_part[...] = col_in[...]
    txts[pl.ds(0, 3 * rows), :] = txts_in[...]
    last = txts.at[pl.ds(3 * rows, rows), :]
    last[...] = unit(t3)
    scores = tiles(logits, NEAR, (3,), rows)
    stats(scale[0], views(near, NEAR, rows), {3: last}, scores, row_part, col_part)


def third_kernel(scale, i2, txts, row_in, col_in, far, logits, row_part, col_part):
    rows = i2.shape[0]
    row_part[...] = row_in[...]
    col_part[...] = col_in[...]
    far[...] = unit(i2)
    blocks = range(SLOTS)
    scores = tiles(logits, (2,), blocks, rows)
    stats(scale[0], {2: far}, views(txts, blocks, rows), scores, row_part, col_part)


def joined(mine, other, bits):
    rows = mine.shape[1] // SLOTS
    swap = lambda at: jnp.concatenate(
        [other[at : at + 1, (k ^ bits) * rows : ((k ^ bits) + 1) * rows] for k in range(SLOTS)],
        axis=1,
    )
    value, mean = merged((mine[0:1, :], mine[1:2, :]), (swap(0), swap(1)))
    return value, mean, mine[2:3, :] + swap(2)


def join_kernel(mine, other, out):
    out[0:1, :], out[1:2, :], out[2:3, :] = joined(mine, other, 1)
    out[3:, :] = jnp.zeros((out.shape[0] - 3, out.shape[1]), jnp.float32)


def slot_sum(v):
    rows = v.shape[1] // SLOTS
    at = [jnp.sum(v[:, k * rows : (k + 1) * rows], axis=1, keepdims=True) for k in range(SLOTS)]
    return (at[0] + at[1]) + (at[2] + at[3])


def lse_kernel(row, row3, col, col2, lse, row_sums, col_sums):
    lane = lax.broadcasted_iota(jnp.int32, row_sums.shape, 1)
    sides = ((joined(row, row3, 3), row_sums), (joined(col, col2, 2), col_sums))
    for at, ((value, mean, matched), out) in enumerate(sides):
        lse[at : at + 1, :] = value
        loss, slope = slot_sum(0.5 * value - matched), slot_sum(0.5 * mean - matched)
        out[...] = jnp.where(lane == 0, loss, jnp.where(lane == 1, slope, 0.0))


def weigh(scores, lse, slots, w, hit=None):
    rows = lse.shape[1] // SLOTS
    diagonal = eye(rows)
    at = lambda k: pl.ds(k * rows, rows)
    for k in slots:
        right = to_column(lse[0:1, at(k)], diagonal)
        for l in range(SLOTS):
            tile = scores[k, l][...]
            weight = 0.5 * (jnp.exp(tile - right) + jnp.exp(tile - lse[1:2, at(l)]))
            if k == 0 and l == 0:
                weight = weight - hit.astype(jnp.float32)
            w[k, l][...] = weight.astype(jnp.bfloat16)


def over(w01, w23, near, far, l):
    rows = far.shape[0]
    span = pl.ds(l * rows, rows)
    term = lambda weights, blocks: lax.dot_general(
        weights, blocks, (((0,), (0,)), ((), ())), preferred_element_type=jnp.float32
    )
    one, two = pl.ds(0, rows), pl.ds(rows, rows)
    return (
        term(w01[:, span], near[pl.ds(0, 2 * rows), :])
        + term(w23[one, span], far[...])
        + term(w23[two, span], near[pl.ds(2 * rows, rows), :])
    )


def weight_kernel(first, second, third, lse, positive, w01, w23):
    rows = w01.shape[0] // 2
    scores = tiles(first, NEAR, (0, 1, 2), rows)
    scores.update(tiles(second, NEAR, (3,), rows))
    scores.update(tiles(third, (2,), range(SLOTS), rows))
    hit = hits(positive, eye(rows))
    weigh(scores, lse, (2, 3), tiles(w23, (2, 3), range(SLOTS), rows))
    weigh(scores, lse, (0, 1), tiles(w01, (0, 1), range(SLOTS), rows), hit)


def early_kernel(w01, w23, near, far, txts, core_part, part2):
    rows = far.shape[0]
    back = jnp.dot(w23[pl.ds(0, rows), :], txts[...], preferred_element_type=jnp.float32)
    part2[...] = back.astype(part2.dtype)
    for n, l in enumerate((1, 3)):
        core_part[pl.ds(n * rows, rows), :] = over(w01, w23, near, far, l).astype(core_part.dtype)


def image_kernel(w01, w23, txts, before, img_back, first, late):
    rows = img_back.shape[0]
    back = lambda w, n: jnp.dot(
        w[pl.ds(n * rows, rows), :], txts[...], preferred_element_type=jnp.float32
    )
    zero = core_index() == 0
    one, three = back(w01, 1), back(w23, 1)
    first[...] = jnp.where(zero, one, three).astype(first.dtype)
    late[...] = jnp.where(zero, three, one)
    img_back[...] = back(w01, 0)


def half_kernel(row, row_core, col, col1, core_in, part2_in, before, sums, core_part, part2):
    sums[...] = jnp.where(core_index() == 0, row[...] + row_core[...], col[...] + col1[...])
    core_part[...] = core_in[...]
    part2[...] = part2_in[...]


def text_kernel(w01, w23, near, far, before, txt_back, txt_next, token):
    token[...] = jnp.zeros(token.shape, jnp.float32)
    for out, l in ((txt_back, 0), (txt_next, 2)):
        out[...] = over(w01, w23, near, far, l)


def across_kernel(txt_next, core_part, first_in, before, part_y, first):
    rows = part_y.shape[0]
    first[...] = first_in[...]
    total = txt_next[...] + core_part[pl.ds(rows, rows), :].astype(jnp.float32)
    part_y[...] = total.astype(part_y.dtype)


def late_kernel(late, relayed, out):
    out[...] = (late[...] + relayed[...].astype(jnp.float32)).astype(out.dtype)


def side_kernel(a, b, before, before_too, out):
    out[...] = a[...] + b[...]


def add_kernel(a, b, out):
    out[...] = a[...] + b[...]


def lane_from_z(shape):
    lane = lax.broadcasted_iota(jnp.int32, shape, 1)
    return (lane - lax.axis_index("dp") // 2 + 8) % 8, lane < 8


def total_kernel(mine, other, held):
    sums = mine[0:1, :] + other[0:1, :]
    line = lax.broadcasted_iota(jnp.int32, held.shape, 0)
    value = jnp.where(line == 0, sums[:, 0:1], jnp.where(line == 1, sums[:, 1:2], 0.0))
    ahead, inside = lane_from_z(held.shape)
    held[...] = jnp.where(inside & (ahead == 0), value, 0.0)


def union(held, other, both):
    ahead, _ = lane_from_z(held.shape)
    twice = functools.reduce(jnp.logical_or, [ahead == n for n in both])
    return jnp.where(twice, held[...], held[...] + other[...])


def planes_kernel(held, other, out):
    out[...] = union(held, other, (0,))


def scalar_kernel(total_rows, scale, held, other, loss, scale_grad):
    sums = jnp.sum(union(held, other, (0, 1, 4, 7)), axis=1, keepdims=True)
    loss[0] = sums[0, 0] / total_rows
    scale_grad[0] = sums[1, 0] / (total_rows * scale[0])


def grad_kernel(scale, image, text, img_back, txt_back, core_part, first, late, py, image_grad, text_grad, token):
    token[...] = jnp.zeros(token.shape, jnp.float32)
    for values, parts, out in (
        (image, (img_back, first, late), image_grad), (text, (txt_back, core_part, py), text_grad),
    ):
        direction, inverse = unit_rows(values[...])
        incoming = scale[0] * sum(
            part[pl.ds(0, direction.shape[0]), :].astype(jnp.float32) for part in parts
        )
        along = jnp.sum(direction * incoming, axis=-1, keepdims=True)
        out[...] = ((incoming - direction * along) * inverse).astype(out.dtype)


def shards(image, text, positive, logit_scale):
    rows, width = image.shape
    group = SLOTS * rows
    f32, bf16 = jnp.float32, jnp.bfloat16
    block, parts = ((rows, width), bf16), ((SLOTS, group), f32)
    positive = positive.reshape(1, rows)

    i1, i3 = swapped(image, X1), swapped(image, X3)
    t1, t2 = swapped(text, CORE), swapped(text, Y)
    own_img, own_txt = call(own_kernel, "own", [block] * 2, image, text)
    (on,) = call(pick_kernel, "pick", [block], i1, i3, own_img)
    i2 = moved(on, relay)
    t3 = swapped(t2, CORE)
    three = group - rows
    near, txts, first, row_part, col_part = call(
        first_kernel, "first", [((three, width), bf16)] * 2 + [((three, three), f32), parts, parts],
        logit_scale, own_img, own_txt, i1, i3, t1, t2, positive, scalar=True,
    )
    txts, second, row_part, col_part = call(
        second_kernel, "second", [((group, width), bf16), ((three, rows), f32), parts, parts],
        logit_scale, t3, near, txts, row_part, col_part, scalar=True,
    )
    few = ((8, 128), f32)
    far, third, row_part, col_part = call(
        third_kernel, "third", [block, ((rows, group), f32), parts, parts],
        logit_scale, i2, txts, row_part, col_part, scalar=True,
    )
    (col_part,) = call(join_kernel, "join", [((2 * SLOTS, group), f32)], col_part, swapped(col_part, CORE))
    col_y = swapped(col_part, Y)
    (row_part,) = call(join_kernel, "join", [parts], row_part, swapped(row_part, X1))
    lse, row_sums, col_sums = call(
        lse_kernel, "lse", [((2, group), f32), few, few],
        row_part, swapped(row_part, X3), col_part, col_y,
    )
    row_core, col1 = swapped(row_sums, CORE), swapped(col_sums, X1)
    heavy = ((2 * rows, group), bf16)
    w01, w23 = call(
        weight_kernel, "weight", [heavy, heavy], first, second, third, lse, positive
    )
    wide = ((rows, width), f32)
    pair = ((2 * rows, width), bf16)
    core_part, part2 = call(early_kernel, "early", [pair, block], w01, w23, near, far, txts)
    sums, core_part, part2 = call(
        half_kernel, "half", [few, pair, block],
        row_sums, row_core, col_sums, col1, core_part, part2, part2,
    )
    core_part, relayed = swapped(core_part, CORE), moved(part2, relay)
    txt_back, txt_next, token = call(
        text_kernel, "text", [wide, wide, few], w01, w23, near, far, sums
    )
    (sums,) = call(side_kernel, "side", [few], sums, swapped(sums, 1, "dp"), token, token)
    sums_got = moved(sums, by_sides)
    img_back, first, late = call(
        image_kernel, "image", [wide, block, wide], w01, w23, txts, sums
    )
    part_y, first = call(
        across_kernel, "across", [block] * 2, txt_next, core_part, first, sums
    )
    (late,) = call(late_kernel, "late", [block], late, relayed)
    (sums,) = call(side_kernel, "side", [few], sums, sums_got, part_y, late)
    part_y, first, late = swapped(part_y, Y), moved(first, relay), moved(late, other_way)
    (held,) = call(total_kernel, "total", [few], sums, swapped(sums, CORE))
    (held,) = call(add_kernel, "add", [few], held, moved(held, by_planes))
    (held,) = call(planes_kernel, "planes", [few], held, swapped(held, CORE))
    image_grad, text_grad, token = call(
        grad_kernel, "grad", [block] * 2 + [few],
        logit_scale, image, text, img_back, txt_back, core_part, first, late, part_y, scalar=True,
    )
    (held,) = call(
        side_kernel, "side", [few], held, moved(held, by_far_planes), token, token
    )
    total_rows = rows * lax.axis_size("blk") * lax.axis_size("dp")
    loss, scale_grad = pl.pallas_call(
        functools.partial(scalar_kernel, total_rows), name="scalar",
        out_shape=[jax.ShapeDtypeStruct((1,), f32)] * 2,
        in_specs=[SMEM, VMEM, VMEM], out_specs=[SMEM] * 2,
        compiler_params=PARAMS,
    )(logit_scale, held, swapped(held, CORE))
    return (loss, scale_grad, image_grad, text_grad)


def solution(mesh):
    in_specs = (P(("dp", "blk"), None), P(("dp", "blk"), None), P(("dp", "blk")), P())
    out_specs = (P(), P(), P(("dp", "blk"), None), P(("dp", "blk"), None))
    return jax.shard_map(shards, mesh=mesh, in_specs=in_specs, out_specs=out_specs, check_vma=False)
```

```python
import functools
import itertools
import math

import jax
import jax.numpy as jnp
from jax import lax
from jax.experimental import pallas as pl
from jax.experimental.pallas import tpu as pltpu
from jax.sharding import PartitionSpec as P

EPSILON = 1e-06
VMEM = pl.BlockSpec(memory_space=pltpu.VMEM)
SMEM = pl.BlockSpec(memory_space=pltpu.SMEM)
PARAMS = pltpu.CompilerParams(vmem_limit_bytes=24 * 1024 * 1024)
SLOTS = 4
LOW = -1e30
COST = {
    "sides": 10, "total": 10,
    "pick": 5.0,
    "own": 0.25, "first": 12, "second": 8, "third": 1.15, "lse": 0.15, "weight": 1.3,
    "image": 1.1, "text": 1.1, "early": 1.4, "half": 0.3, "across": 0.2, "late": 0.2, "grad": 1.6,
}
NEAR = (0, 1, 3)
X1, X2, X3, Y, CORE = 4, 8, 12, 2, 1


def swapped(value, bits, axis="blk"):
    return lax.ppermute(value, axis, [(i, i ^ bits) for i in range(lax.axis_size(axis))])


def moved(value, step):
    places = itertools.product(range(8), range(2), range(4), range(2), range(2))
    flat = lambda z, lo, x, hi, core: (z % 8 * 2 + lo) * 16 + x * 4 + hi * 2 + core
    pairs = [(flat(*p), flat(*step(*p))) for p in places]
    return lax.ppermute(value, ("dp", "blk"), pairs)


def by_sides(z, lo, x, hi, core):
    return (z, 1 - lo, x, 1 - hi, core) if core == 0 else (z, lo, 3 - x, hi, core)


def relay(z, lo, x, hi, core):
    return (z, lo, x ^ 1 if core == 0 else 3 - x, hi, core)


def other_way(z, lo, x, hi, core):
    return (z, lo, 3 - x if core == 0 else x ^ 1, hi, core)


def by_planes(z, lo, x, hi, core):
    return (z + (1 if (z + core) % 2 == 0 else -1), lo, x, hi, core)


def by_far_planes(z, lo, x, hi, core):
    return (z + (-3 if core == 0 else 3), lo, x, hi, core)


def call(kernel, name, outs, *args, scalar=False):
    specs = [SMEM] * scalar + [VMEM] * (len(args) - scalar)
    moved = sum(a.size * a.dtype.itemsize for a in args)
    moved += sum(math.prod(s) * jnp.dtype(d).itemsize for s, d in outs)
    return pl.pallas_call(
        kernel, out_shape=[jax.ShapeDtypeStruct(s, d) for s, d in outs], in_specs=specs,
        out_specs=[VMEM] * len(outs), name=name,
        cost_estimate=pl.CostEstimate(
            flops=int(COST.get(name, 0.05) * 1.1e9), bytes_accessed=moved, transcendentals=0
        ),
        compiler_params=PARAMS,
    )(*args)


def eye(n):
    return lax.broadcasted_iota(jnp.int32, (n, n), 0) == lax.broadcasted_iota(jnp.int32, (n, n), 1)


def to_row(column, diagonal):
    return jnp.sum(jnp.where(diagonal, column, 0.0), axis=0, keepdims=True)


def to_column(row, diagonal):
    return jnp.sum(jnp.where(diagonal, row, 0.0), axis=1, keepdims=True)


def unit_rows(values):
    wide = values.astype(jnp.float32)
    inverse = lax.rsqrt(jnp.sum(wide * wide, axis=-1, keepdims=True) + EPSILON)
    return wide * inverse, inverse


def hits(positive, diagonal):
    target = to_column(positive[...].astype(jnp.float32), diagonal).astype(jnp.int32)
    return lax.broadcasted_iota(jnp.int32, diagonal.shape, 1) == target


def merged(a, b):
    top = jnp.maximum(a[0], b[0])
    ea, eb = jnp.exp(a[0] - top), jnp.exp(b[0] - top)
    both = ea + eb
    return top + jnp.log(both), (a[1] * ea + b[1] * eb) / both


def into(part, span, value):
    part[0:1, span], part[1:2, span] = merged((part[0:1, span], part[1:2, span]), value)


def stats(scale, imgs, txts, logits, row_part, col_part):
    diagonal = eye(next(iter(txts.values())).shape[0])
    rows = diagonal.shape[0]
    slots, blocks = tuple(imgs), tuple(txts)
    at = lambda k: pl.ds(k * rows, rows)
    row_top, col_top = {}, {}
    for l in blocks:
        for k in slots:
            tile = scale * lax.dot_general(
                imgs[k][...], txts[l][...], (((1,), (1,)), ((), ())),
                preferred_element_type=jnp.float32,
            )
            logits[k, l][...] = tile
            right = jnp.max(tile, axis=1, keepdims=True)
            down = jnp.max(tile, axis=0, keepdims=True)
            row_top[k] = jnp.maximum(row_top[k], right) if k in row_top else right
            col_top[l] = jnp.maximum(col_top[l], down) if l in col_top else down
    none = jnp.zeros((1, rows), jnp.float32)
    col_sum, col_moment = {l: none for l in blocks}, {l: none for l in blocks}
    for k in slots:
        total = jnp.zeros((rows, 1), jnp.float32)
        moment = jnp.zeros((rows, 1), jnp.float32)
        for l in blocks:
            tile = logits[k, l][...]
            e = jnp.exp(tile - row_top[k])
            total += jnp.sum(e, axis=1, keepdims=True)
            moment += jnp.sum(e * tile, axis=1, keepdims=True)
            f = jnp.exp(tile - col_top[l])
            col_sum[l] += jnp.sum(f, axis=0, keepdims=True)
            col_moment[l] += jnp.sum(f * tile, axis=0, keepdims=True)
        total = to_row(total, diagonal)
        top = to_row(row_top[k], diagonal)
        into(row_part, at(k), (top + jnp.log(total), to_row(moment, diagonal) / total))
    for l in blocks:
        into(col_part, at(l), (col_top[l] + jnp.log(col_sum[l]), col_moment[l] / col_sum[l]))


def unit(values):
    return unit_rows(values[...])[0].astype(jnp.bfloat16)


def views(ref, slots, rows):
    return {k: ref.at[pl.ds(n * rows, rows), :] for n, k in enumerate(slots)}


def tiles(ref, slots, blocks, rows):
    return {
        (k, l): ref.at[pl.ds(n * rows, rows), pl.ds(m * rows, rows)]
        for n, k in enumerate(slots) for m, l in enumerate(blocks)
    }


def own_kernel(image, text, img_unit, txt_unit):
    img_unit[...] = unit(image)
    txt_unit[...] = unit(text)


def first_kernel(
    scale, i0, t0, i1, i3, t1, t2, positive, near, txts, logits, row_part, col_part
):
    rows = i0.shape[0]
    imgs, texts = views(near, NEAR, rows), views(txts, (0, 1, 2), rows)
    imgs[0][...] = i0[...]
    texts[0][...] = t0[...]
    imgs[1][...], imgs[3][...] = unit(i1), unit(i3)
    texts[1][...], texts[2][...] = unit(t1), unit(t2)
    for part in (row_part, col_part):
        part[0:1, :] = jnp.full((1, SLOTS * rows), LOW, jnp.float32)
        part[1:4, :] = jnp.zeros((3, SLOTS * rows), jnp.float32)
    scores = tiles(logits, NEAR, (0, 1, 2), rows)
    stats(scale[0], imgs, texts, scores, row_part, col_part)
    matched = jnp.where(hits(positive, eye(rows)), scores[0, 0][...], 0.0)
    row_part[2:3, pl.ds(0, rows)] = jnp.sum(matched, axis=0, keepdims=True)


def core_index():
    return lax.axis_index("blk") % 2


def pick_kernel(i1, i3, before, out):
    core = core_index()

    @pl.when(core == 0)
    def _():
        out[...] = i3[...]

    @pl.when(core != 0)
    def _():
        out[...] = i1[...]


def second_kernel(scale, t3, near, txts_in, row_in, col_in, txts, logits, row_part, col_part):
    rows = t3.shape[0]
    row_part[...] = row_in[...]
    col_part[...] = col_in[...]
    txts[pl.ds(0, 3 * rows), :] = txts_in[...]
    last = txts.at[pl.ds(3 * rows, rows), :]
    last[...] = unit(t3)
    scores = tiles(logits, NEAR, (3,), rows)
    stats(scale[0], views(near, NEAR, rows), {3: last}, scores, row_part, col_part)


def third_kernel(scale, i2, txts, row_in, col_in, far, logits, row_part, col_part):
    rows = i2.shape[0]
    row_part[...] = row_in[...]
    col_part[...] = col_in[...]
    far[...] = unit(i2)
    blocks = range(SLOTS)
    scores = tiles(logits, (2,), blocks, rows)
    stats(scale[0], {2: far}, views(txts, blocks, rows), scores, row_part, col_part)


def joined(mine, other, bits):
    rows = mine.shape[1] // SLOTS
    swap = lambda at: jnp.concatenate(
        [other[at : at + 1, (k ^ bits) * rows : ((k ^ bits) + 1) * rows] for k in range(SLOTS)],
        axis=1,
    )
    value, mean = merged((mine[0:1, :], mine[1:2, :]), (swap(0), swap(1)))
    return value, mean, mine[2:3, :] + swap(2)


def join_kernel(mine, other, out):
    out[0:1, :], out[1:2, :], out[2:3, :] = joined(mine, other, 1)
    out[3:, :] = jnp.zeros((out.shape[0] - 3, out.shape[1]), jnp.float32)


def slot_sum(v):
    rows = v.shape[1] // SLOTS
    at = [jnp.sum(v[:, k * rows : (k + 1) * rows], axis=1, keepdims=True) for k in range(SLOTS)]
    return (at[0] + at[1]) + (at[2] + at[3])


def lse_kernel(row, row3, col, col2, lse, row_sums, col_sums):
    lane = lax.broadcasted_iota(jnp.int32, row_sums.shape, 1)
    sides = ((joined(row, row3, 3), row_sums), (joined(col, col2, 2), col_sums))
    for at, ((value, mean, matched), out) in enumerate(sides):
        lse[at : at + 1, :] = value
        loss, slope = slot_sum(0.5 * value - matched), slot_sum(0.5 * mean - matched)
        out[...] = jnp.where(lane == 0, loss, jnp.where(lane == 1, slope, 0.0))


def weigh(scores, lse, slots, w, hit=None):
    rows = lse.shape[1] // SLOTS
    diagonal = eye(rows)
    at = lambda k: pl.ds(k * rows, rows)
    for k in slots:
        right = to_column(lse[0:1, at(k)], diagonal)
        for l in range(SLOTS):
            tile = scores[k, l][...]
            weight = 0.5 * (jnp.exp(tile - right) + jnp.exp(tile - lse[1:2, at(l)]))
            if k == 0 and l == 0:
                weight = weight - hit.astype(jnp.float32)
            w[k, l][...] = weight.astype(jnp.bfloat16)


def over(w01, w23, near, far, l):
    rows = far.shape[0]
    span = pl.ds(l * rows, rows)
    term = lambda weights, blocks: lax.dot_general(
        weights, blocks, (((0,), (0,)), ((), ())), preferred_element_type=jnp.float32
    )
    one, two = pl.ds(0, rows), pl.ds(rows, rows)
    return (
        term(w01[:, span], near[pl.ds(0, 2 * rows), :])
        + term(w23[one, span], far[...])
        + term(w23[two, span], near[pl.ds(2 * rows, rows), :])
    )


def weight_kernel(first, second, third, lse, positive, w01, w23):
    rows = w01.shape[0] // 2
    scores = tiles(first, NEAR, (0, 1, 2), rows)
    scores.update(tiles(second, NEAR, (3,), rows))
    scores.update(tiles(third, (2,), range(SLOTS), rows))
    hit = hits(positive, eye(rows))
    weigh(scores, lse, (2, 3), tiles(w23, (2, 3), range(SLOTS), rows))
    weigh(scores, lse, (0, 1), tiles(w01, (0, 1), range(SLOTS), rows), hit)


def early_kernel(w01, w23, near, far, txts, core_part, part2):
    rows = far.shape[0]
    back = jnp.dot(w23[pl.ds(0, rows), :], txts[...], preferred_element_type=jnp.float32)
    part2[...] = back.astype(part2.dtype)
    for n, l in enumerate((1, 3)):
        core_part[pl.ds(n * rows, rows), :] = over(w01, w23, near, far, l).astype(core_part.dtype)


def image_kernel(w01, w23, txts, before, img_back, first, late):
    rows = img_back.shape[0]
    back = lambda w, n: jnp.dot(
        w[pl.ds(n * rows, rows), :], txts[...], preferred_element_type=jnp.float32
    )
    zero = core_index() == 0
    one, three = back(w01, 1), back(w23, 1)
    first[...] = jnp.where(zero, one, three).astype(first.dtype)
    late[...] = jnp.where(zero, three, one)
    img_back[...] = back(w01, 0)


def half_kernel(row, row_core, col, col1, core_in, part2_in, before, sums, core_part, part2):
    sums[...] = jnp.where(core_index() == 0, row[...] + row_core[...], col[...] + col1[...])
    core_part[...] = core_in[...]
    part2[...] = part2_in[...]


def text_kernel(w01, w23, near, far, before, txt_back, txt_next, token):
    token[...] = jnp.zeros(token.shape, jnp.float32)
    for out, l in ((txt_back, 0), (txt_next, 2)):
        out[...] = over(w01, w23, near, far, l)


def across_kernel(txt_next, core_part, first_in, before, part_y, first):
    rows = part_y.shape[0]
    first[...] = first_in[...]
    total = txt_next[...] + core_part[pl.ds(rows, rows), :].astype(jnp.float32)
    part_y[...] = total.astype(part_y.dtype)


def late_kernel(late, relayed, before, out):
    out[...] = (late[...] + relayed[...].astype(jnp.float32)).astype(out.dtype)


def side_kernel(a, b, before, before_too, out):
    out[...] = a[...] + b[...]


def add_kernel(a, b, out):
    out[...] = a[...] + b[...]


def lane_from_z(shape):
    lane = lax.broadcasted_iota(jnp.int32, shape, 1)
    return (lane - lax.axis_index("dp") // 2 + 8) % 8, lane < 8


def total_kernel(mine, other, before, held):
    sums = mine[0:1, :] + other[0:1, :]
    line = lax.broadcasted_iota(jnp.int32, held.shape, 0)
    value = jnp.where(line == 0, sums[:, 0:1], jnp.where(line == 1, sums[:, 1:2], 0.0))
    ahead, inside = lane_from_z(held.shape)
    held[...] = jnp.where(inside & (ahead == 0), value, 0.0)


def union(held, other, both):
    ahead, _ = lane_from_z(held.shape)
    twice = functools.reduce(jnp.logical_or, [ahead == n for n in both])
    return jnp.where(twice, held[...], held[...] + other[...])


def planes_kernel(held, other, out):
    out[...] = union(held, other, (0,))


def scalar_kernel(total_rows, scale, held, other, loss, scale_grad):
    sums = jnp.sum(union(held, other, (0, 1, 4, 7)), axis=1, keepdims=True)
    loss[0] = sums[0, 0] / total_rows
    scale_grad[0] = sums[1, 0] / (total_rows * scale[0])


def grad_kernel(scale, image, text, img_back, txt_back, core_part, first, late, py, image_grad, text_grad, token):
    token[...] = jnp.zeros(token.shape, jnp.float32)
    for values, parts, out in (
        (image, (img_back, first, late), image_grad), (text, (txt_back, core_part, py), text_grad),
    ):
        direction, inverse = unit_rows(values[...])
        incoming = scale[0] * sum(
            part[pl.ds(0, direction.shape[0]), :].astype(jnp.float32) for part in parts
        )
        along = jnp.sum(direction * incoming, axis=-1, keepdims=True)
        out[...] = ((incoming - direction * along) * inverse).astype(out.dtype)


def shards(image, text, positive, logit_scale):
    rows, width = image.shape
    group = SLOTS * rows
    f32, bf16 = jnp.float32, jnp.bfloat16
    block, parts = ((rows, width), bf16), ((SLOTS, group), f32)
    positive = positive.reshape(1, rows)

    i1, i3 = swapped(image, X1), swapped(image, X3)
    t1, t2 = swapped(text, CORE), swapped(text, Y)
    own_img, own_txt = call(own_kernel, "own", [block] * 2, image, text)
    (on,) = call(pick_kernel, "pick", [block], i1, i3, own_img)
    i2 = moved(on, relay)
    t3 = swapped(t2, CORE)
    three = group - rows
    near, txts, first, row_part, col_part = call(
        first_kernel, "first", [((three, width), bf16)] * 2 + [((three, three), f32), parts, parts],
        logit_scale, own_img, own_txt, i1, i3, t1, t2, positive, scalar=True,
    )
    txts, second, row_part, col_part = call(
        second_kernel, "second", [((group, width), bf16), ((three, rows), f32), parts, parts],
        logit_scale, t3, near, txts, row_part, col_part, scalar=True,
    )
    few = ((8, 128), f32)
    far, third, row_part, col_part = call(
        third_kernel, "third", [block, ((rows, group), f32), parts, parts],
        logit_scale, i2, txts, row_part, col_part, scalar=True,
    )
    (col_part,) = call(join_kernel, "join", [((2 * SLOTS, group), f32)], col_part, swapped(col_part, CORE))
    col_y = swapped(col_part, Y)
    (row_part,) = call(join_kernel, "join", [parts], row_part, swapped(row_part, X1))
    lse, row_sums, col_sums = call(
        lse_kernel, "lse", [((2, group), f32), few, few],
        row_part, swapped(row_part, X3), col_part, col_y,
    )
    row_core, col1 = swapped(row_sums, CORE), swapped(col_sums, X1)
    heavy = ((2 * rows, group), bf16)
    w01, w23 = call(
        weight_kernel, "weight", [heavy, heavy], first, second, third, lse, positive
    )
    wide = ((rows, width), f32)
    pair = ((2 * rows, width), bf16)
    core_part, part2 = call(early_kernel, "early", [pair, block], w01, w23, near, far, txts)
    sums, core_part, part2 = call(
        half_kernel, "half", [few, pair, block],
        row_sums, row_core, col_sums, col1, core_part, part2, part2,
    )
    core_part, relayed = swapped(core_part, CORE), moved(part2, relay)
    txt_back, txt_next, token = call(
        text_kernel, "text", [wide, wide, few], w01, w23, near, far, sums
    )
    img_back, first, late = call(
        image_kernel, "image", [wide, block, wide], w01, w23, txts, sums
    )
    (sums,) = call(side_kernel, "side", [few], sums, swapped(sums, 1, "dp"), token, late)
    sums_got = moved(sums, by_sides)
    part_y, first = call(
        across_kernel, "across", [block] * 2, txt_next, core_part, first, sums
    )
    (sums,) = call(side_kernel, "sides", [few], sums, sums_got, part_y, relayed)
    part_y, first = swapped(part_y, Y), moved(first, relay)
    (late,) = call(late_kernel, "late", [block], late, relayed, sums)
    (held,) = call(total_kernel, "total", [few], sums, swapped(sums, CORE), late)
    late = moved(late, other_way)
    (held,) = call(add_kernel, "add", [few], held, moved(held, by_planes))
    (held,) = call(planes_kernel, "planes", [few], held, swapped(held, CORE))
    image_grad, text_grad, token = call(
        grad_kernel, "grad", [block] * 2 + [few],
        logit_scale, image, text, img_back, txt_back, core_part, first, late, part_y, scalar=True,
    )
    (held,) = call(
        side_kernel, "side", [few], held, moved(held, by_far_planes), token, token
    )
    total_rows = rows * lax.axis_size("blk") * lax.axis_size("dp")
    loss, scale_grad = pl.pallas_call(
        functools.partial(scalar_kernel, total_rows), name="scalar",
        out_shape=[jax.ShapeDtypeStruct((1,), f32)] * 2,
        in_specs=[SMEM, VMEM, VMEM], out_specs=[SMEM] * 2,
        compiler_params=PARAMS,
    )(logit_scale, held, swapped(held, CORE))
    return (loss, scale_grad, image_grad, text_grad)


def solution(mesh):
    in_specs = (P(("dp", "blk"), None), P(("dp", "blk"), None), P(("dp", "blk")), P())
    out_specs = (P(), P(), P(("dp", "blk"), None), P(("dp", "blk"), None))
    return jax.shard_map(shards, mesh=mesh, in_specs=in_specs, out_specs=out_specs, check_vma=False)
```

```python
import functools
import itertools
import math

import jax
import jax.numpy as jnp
from jax import lax
from jax.experimental import pallas as pl
from jax.experimental.pallas import tpu as pltpu
from jax.sharding import PartitionSpec as P

EPSILON = 1e-06
VMEM = pl.BlockSpec(memory_space=pltpu.VMEM)
SMEM = pl.BlockSpec(memory_space=pltpu.SMEM)
PARAMS = pltpu.CompilerParams(vmem_limit_bytes=24 * 1024 * 1024)
SLOTS = 4
LOW = -1e30
COST = {
    "sides": 10, "total": 10,
    "pick": 5.0,
    "own": 0.25, "first": 12, "second": 8, "third": 1.15, "lse": 0.15, "weight": 1.3,
    "image": 1.1, "text": 1.1, "early": 1.4, "half": 0.3, "across": 0.2, "late": 0.2, "text_grad": 0.8, "image_grad": 0.8,
}
NEAR = (0, 1, 3)
X1, X2, X3, Y, CORE = 4, 8, 12, 2, 1


def swapped(value, bits, axis="blk"):
    return lax.ppermute(value, axis, [(i, i ^ bits) for i in range(lax.axis_size(axis))])


def moved(value, step):
    places = itertools.product(range(8), range(2), range(4), range(2), range(2))
    flat = lambda z, lo, x, hi, core: (z % 8 * 2 + lo) * 16 + x * 4 + hi * 2 + core
    pairs = [(flat(*p), flat(*step(*p))) for p in places]
    return lax.ppermute(value, ("dp", "blk"), pairs)


def by_sides(z, lo, x, hi, core):
    return (z, 1 - lo, x, 1 - hi, core) if core == 0 else (z, lo, 3 - x, hi, core)


def relay(z, lo, x, hi, core):
    return (z, lo, x ^ 1 if core == 0 else 3 - x, hi, core)


def other_way(z, lo, x, hi, core):
    return (z, lo, 3 - x if core == 0 else x ^ 1, hi, core)


def by_planes(z, lo, x, hi, core):
    return (z + (1 if (z + core) % 2 == 0 else -1), lo, x, hi, core)


def by_far_planes(z, lo, x, hi, core):
    return (z + (-3 if core == 0 else 3), lo, x, hi, core)


def call(kernel, name, outs, *args, scalar=False):
    specs = [SMEM] * scalar + [VMEM] * (len(args) - scalar)
    moved = sum(a.size * a.dtype.itemsize for a in args)
    moved += sum(math.prod(s) * jnp.dtype(d).itemsize for s, d in outs)
    return pl.pallas_call(
        kernel, out_shape=[jax.ShapeDtypeStruct(s, d) for s, d in outs], in_specs=specs,
        out_specs=[VMEM] * len(outs), name=name,
        cost_estimate=pl.CostEstimate(
            flops=int(COST.get(name, 0.05) * 1.1e9), bytes_accessed=moved, transcendentals=0
        ),
        compiler_params=PARAMS,
    )(*args)


def eye(n):
    return lax.broadcasted_iota(jnp.int32, (n, n), 0) == lax.broadcasted_iota(jnp.int32, (n, n), 1)


def to_row(column, diagonal):
    return jnp.sum(jnp.where(diagonal, column, 0.0), axis=0, keepdims=True)


def to_column(row, diagonal):
    return jnp.sum(jnp.where(diagonal, row, 0.0), axis=1, keepdims=True)


def unit_rows(values):
    wide = values.astype(jnp.float32)
    inverse = lax.rsqrt(jnp.sum(wide * wide, axis=-1, keepdims=True) + EPSILON)
    return wide * inverse, inverse


def hits(positive, diagonal):
    target = to_column(positive[...].astype(jnp.float32), diagonal).astype(jnp.int32)
    return lax.broadcasted_iota(jnp.int32, diagonal.shape, 1) == target


def merged(a, b):
    top = jnp.maximum(a[0], b[0])
    ea, eb = jnp.exp(a[0] - top), jnp.exp(b[0] - top)
    both = ea + eb
    return top + jnp.log(both), (a[1] * ea + b[1] * eb) / both


def into(part, span, value):
    part[0:1, span], part[1:2, span] = merged((part[0:1, span], part[1:2, span]), value)


def stats(scale, imgs, txts, logits, row_part, col_part):
    diagonal = eye(next(iter(txts.values())).shape[0])
    rows = diagonal.shape[0]
    slots, blocks = tuple(imgs), tuple(txts)
    at = lambda k: pl.ds(k * rows, rows)
    row_top, col_top = {}, {}
    for l in blocks:
        for k in slots:
            tile = scale * lax.dot_general(
                imgs[k][...], txts[l][...], (((1,), (1,)), ((), ())),
                preferred_element_type=jnp.float32,
            )
            logits[k, l][...] = tile
            right = jnp.max(tile, axis=1, keepdims=True)
            down = jnp.max(tile, axis=0, keepdims=True)
            row_top[k] = jnp.maximum(row_top[k], right) if k in row_top else right
            col_top[l] = jnp.maximum(col_top[l], down) if l in col_top else down
    none = jnp.zeros((1, rows), jnp.float32)
    col_sum, col_moment = {l: none for l in blocks}, {l: none for l in blocks}
    for k in slots:
        total = jnp.zeros((rows, 1), jnp.float32)
        moment = jnp.zeros((rows, 1), jnp.float32)
        for l in blocks:
            tile = logits[k, l][...]
            e = jnp.exp(tile - row_top[k])
            total += jnp.sum(e, axis=1, keepdims=True)
            moment += jnp.sum(e * tile, axis=1, keepdims=True)
            f = jnp.exp(tile - col_top[l])
            col_sum[l] += jnp.sum(f, axis=0, keepdims=True)
            col_moment[l] += jnp.sum(f * tile, axis=0, keepdims=True)
        total = to_row(total, diagonal)
        top = to_row(row_top[k], diagonal)
        into(row_part, at(k), (top + jnp.log(total), to_row(moment, diagonal) / total))
    for l in blocks:
        into(col_part, at(l), (col_top[l] + jnp.log(col_sum[l]), col_moment[l] / col_sum[l]))


def unit(values):
    return unit_rows(values[...])[0].astype(jnp.bfloat16)


def views(ref, slots, rows):
    return {k: ref.at[pl.ds(n * rows, rows), :] for n, k in enumerate(slots)}


def tiles(ref, slots, blocks, rows):
    return {
        (k, l): ref.at[pl.ds(n * rows, rows), pl.ds(m * rows, rows)]
        for n, k in enumerate(slots) for m, l in enumerate(blocks)
    }


def own_kernel(image, text, img_unit, txt_unit):
    img_unit[...] = unit(image)
    txt_unit[...] = unit(text)


def first_kernel(
    scale, i0, t0, i1, i3, t1, t2, positive, near, txts, logits, row_part, col_part
):
    rows = i0.shape[0]
    imgs, texts = views(near, NEAR, rows), views(txts, (0, 1, 2), rows)
    imgs[0][...] = i0[...]
    texts[0][...] = t0[...]
    imgs[1][...], imgs[3][...] = unit(i1), unit(i3)
    texts[1][...], texts[2][...] = unit(t1), unit(t2)
    for part in (row_part, col_part):
        part[0:1, :] = jnp.full((1, SLOTS * rows), LOW, jnp.float32)
        part[1:4, :] = jnp.zeros((3, SLOTS * rows), jnp.float32)
    scores = tiles(logits, NEAR, (0, 1, 2), rows)
    stats(scale[0], imgs, texts, scores, row_part, col_part)
    matched = jnp.where(hits(positive, eye(rows)), scores[0, 0][...], 0.0)
    row_part[2:3, pl.ds(0, rows)] = jnp.sum(matched, axis=0, keepdims=True)


def core_index():
    return lax.axis_index("blk") % 2


def pick_kernel(i1, i3, before, out):
    core = core_index()

    @pl.when(core == 0)
    def _():
        out[...] = i3[...]

    @pl.when(core != 0)
    def _():
        out[...] = i1[...]


def second_kernel(scale, t3, near, txts_in, row_in, col_in, txts, logits, row_part, col_part):
    rows = t3.shape[0]
    row_part[...] = row_in[...]
    col_part[...] = col_in[...]
    txts[pl.ds(0, 3 * rows), :] = txts_in[...]
    last = txts.at[pl.ds(3 * rows, rows), :]
    last[...] = unit(t3)
    scores = tiles(logits, NEAR, (3,), rows)
    stats(scale[0], views(near, NEAR, rows), {3: last}, scores, row_part, col_part)


def third_kernel(scale, i2, txts, row_in, col_in, far, logits, row_part, col_part):
    rows = i2.shape[0]
    row_part[...] = row_in[...]
    col_part[...] = col_in[...]
    far[...] = unit(i2)
    blocks = range(SLOTS)
    scores = tiles(logits, (2,), blocks, rows)
    stats(scale[0], {2: far}, views(txts, blocks, rows), scores, row_part, col_part)


def joined(mine, other, bits):
    rows = mine.shape[1] // SLOTS
    swap = lambda at: jnp.concatenate(
        [other[at : at + 1, (k ^ bits) * rows : ((k ^ bits) + 1) * rows] for k in range(SLOTS)],
        axis=1,
    )
    value, mean = merged((mine[0:1, :], mine[1:2, :]), (swap(0), swap(1)))
    return value, mean, mine[2:3, :] + swap(2)


def join_kernel(bits, mine, other, out):
    out[0:1, :], out[1:2, :], out[2:3, :] = joined(mine, other, bits)
    out[3:, :] = jnp.zeros((out.shape[0] - 3, out.shape[1]), jnp.float32)


def slot_sum(v):
    rows = v.shape[1] // SLOTS
    at = [jnp.sum(v[:, k * rows : (k + 1) * rows], axis=1, keepdims=True) for k in range(SLOTS)]
    return (at[0] + at[1]) + (at[2] + at[3])


def lse_kernel(row, row1, col, col2, lse, row_sums, col_sums):
    lane = lax.broadcasted_iota(jnp.int32, row_sums.shape, 1)
    sides = ((joined(row, row1, 1), row_sums), (joined(col, col2, 2), col_sums))
    for at, ((value, mean, matched), out) in enumerate(sides):
        lse[at : at + 1, :] = value
        loss, slope = slot_sum(0.5 * value - matched), slot_sum(0.5 * mean - matched)
        out[...] = jnp.where(lane == 0, loss, jnp.where(lane == 1, slope, 0.0))


def weigh(scores, lse, slots, w, hit=None):
    rows = lse.shape[1] // SLOTS
    diagonal = eye(rows)
    at = lambda k: pl.ds(k * rows, rows)
    for k in slots:
        right = to_column(lse[0:1, at(k)], diagonal)
        for l in range(SLOTS):
            tile = scores[k, l][...]
            weight = 0.5 * (jnp.exp(tile - right) + jnp.exp(tile - lse[1:2, at(l)]))
            if k == 0 and l == 0:
                weight = weight - hit.astype(jnp.float32)
            w[k, l][...] = weight.astype(jnp.bfloat16)


def over(w01, w23, near, far, l):
    rows = far.shape[0]
    span = pl.ds(l * rows, rows)
    term = lambda weights, blocks: lax.dot_general(
        weights, blocks, (((0,), (0,)), ((), ())), preferred_element_type=jnp.float32
    )
    one, two = pl.ds(0, rows), pl.ds(rows, rows)
    return (
        term(w01[:, span], near[pl.ds(0, 2 * rows), :])
        + term(w23[one, span], far[...])
        + term(w23[two, span], near[pl.ds(2 * rows, rows), :])
    )


def weight_kernel(first, second, third, lse, positive, w01, w23):
    rows = w01.shape[0] // 2
    scores = tiles(first, NEAR, (0, 1, 2), rows)
    scores.update(tiles(second, NEAR, (3,), rows))
    scores.update(tiles(third, (2,), range(SLOTS), rows))
    hit = hits(positive, eye(rows))
    weigh(scores, lse, (2, 3), tiles(w23, (2, 3), range(SLOTS), rows))
    weigh(scores, lse, (0, 1), tiles(w01, (0, 1), range(SLOTS), rows), hit)


def early_kernel(w01, w23, near, far, txts, core_part, part2):
    rows = far.shape[0]
    back = jnp.dot(w23[pl.ds(0, rows), :], txts[...], preferred_element_type=jnp.float32)
    part2[...] = back.astype(part2.dtype)
    for n, l in enumerate((1, 3)):
        core_part[pl.ds(n * rows, rows), :] = over(w01, w23, near, far, l).astype(core_part.dtype)


def image_kernel(w01, w23, txts, before, img_back, first, late):
    rows = img_back.shape[0]
    back = lambda w, n: jnp.dot(
        w[pl.ds(n * rows, rows), :], txts[...], preferred_element_type=jnp.float32
    )
    zero = core_index() == 0
    one, three = back(w01, 1), back(w23, 1)
    first[...] = jnp.where(zero, one, three).astype(first.dtype)
    late[...] = jnp.where(zero, three, one)
    img_back[...] = back(w01, 0)


def half_kernel(row, row_core, col, col1, core_in, part2_in, before, sums, core_part, part2):
    sums[...] = jnp.where(core_index() == 0, row[...] + row_core[...], col[...] + col1[...])
    core_part[...] = core_in[...]
    part2[...] = part2_in[...]


def text_kernel(w01, w23, near, far, before, txt_back, txt_next, token):
    token[...] = jnp.zeros(token.shape, jnp.float32)
    for out, l in ((txt_back, 0), (txt_next, 2)):
        out[...] = over(w01, w23, near, far, l)


def across_kernel(txt_next, core_part, first_in, before, part_y, first):
    rows = part_y.shape[0]
    first[...] = first_in[...]
    total = txt_next[...] + core_part[pl.ds(rows, rows), :].astype(jnp.float32)
    part_y[...] = total.astype(part_y.dtype)


def late_kernel(late, relayed, before, out):
    out[...] = (late[...] + relayed[...].astype(jnp.float32)).astype(out.dtype)


def side_kernel(a, b, before, before_too, out):
    out[...] = a[...] + b[...]


def add_kernel(a, b, out):
    out[...] = a[...] + b[...]


def lane_from_z(shape):
    lane = lax.broadcasted_iota(jnp.int32, shape, 1)
    return (lane - lax.axis_index("dp") // 2 + 8) % 8, lane < 8


def total_kernel(mine, other, before, held):
    sums = mine[0:1, :] + other[0:1, :]
    line = lax.broadcasted_iota(jnp.int32, held.shape, 0)
    value = jnp.where(line == 0, sums[:, 0:1], jnp.where(line == 1, sums[:, 1:2], 0.0))
    ahead, inside = lane_from_z(held.shape)
    held[...] = jnp.where(inside & (ahead == 0), value, 0.0)


def union(held, other, both):
    ahead, _ = lane_from_z(held.shape)
    twice = functools.reduce(jnp.logical_or, [ahead == n for n in both])
    return jnp.where(twice, held[...], held[...] + other[...])


def planes_kernel(held, other, out):
    out[...] = union(held, other, (0,))


def scalar_kernel(total_rows, scale, held, other, before, loss, scale_grad):
    sums = jnp.sum(union(held, other, (0, 1, 4, 7)), axis=1, keepdims=True)
    loss[0] = sums[0, 0] / total_rows
    scale_grad[0] = sums[1, 0] / (total_rows * scale[0])


def grad_kernel(scale, values, *refs):
    parts, out, token = refs[:-2], refs[-2], refs[-1]
    token[...] = jnp.zeros(token.shape, jnp.float32)
    direction, inverse = unit_rows(values[...])
    incoming = scale[0] * sum(
        part[pl.ds(0, direction.shape[0]), :].astype(jnp.float32) for part in parts
    )
    along = jnp.sum(direction * incoming, axis=-1, keepdims=True)
    out[...] = ((incoming - direction * along) * inverse).astype(out.dtype)


def shards(image, text, positive, logit_scale):
    rows, width = image.shape
    group = SLOTS * rows
    f32, bf16 = jnp.float32, jnp.bfloat16
    block, parts = ((rows, width), bf16), ((SLOTS, group), f32)
    positive = positive.reshape(1, rows)

    i1, i3 = swapped(image, X1), swapped(image, X3)
    t1, t2 = swapped(text, CORE), swapped(text, Y)
    own_img, own_txt = call(own_kernel, "own", [block] * 2, image, text)
    (on,) = call(pick_kernel, "pick", [block], i1, i3, own_img)
    i2 = moved(on, relay)
    t3 = swapped(t2, CORE)
    three = group - rows
    near, txts, first, row_part, col_part = call(
        first_kernel, "first", [((three, width), bf16)] * 2 + [((three, three), f32), parts, parts],
        logit_scale, own_img, own_txt, i1, i3, t1, t2, positive, scalar=True,
    )
    txts, second, row_part, col_part = call(
        second_kernel, "second", [((group, width), bf16), ((three, rows), f32), parts, parts],
        logit_scale, t3, near, txts, row_part, col_part, scalar=True,
    )
    few = ((8, 128), f32)
    far, third, row_part, col_part = call(
        third_kernel, "third", [block, ((rows, group), f32), parts, parts],
        logit_scale, i2, txts, row_part, col_part, scalar=True,
    )
    (col_part,) = call(
        functools.partial(join_kernel, 1), "join", [((2 * SLOTS, group), f32)],
        col_part, swapped(col_part, CORE),
    )
    col_y = swapped(col_part, Y)
    (row_part,) = call(
        functools.partial(join_kernel, 3), "join", [parts], row_part, swapped(row_part, X3)
    )
    lse, row_sums, col_sums = call(
        lse_kernel, "lse", [((2, group), f32), few, few],
        row_part, swapped(row_part, X1), col_part, col_y,
    )
    row_core, col1 = swapped(row_sums, CORE), swapped(col_sums, X1)
    heavy = ((2 * rows, group), bf16)
    w01, w23 = call(
        weight_kernel, "weight", [heavy, heavy], first, second, third, lse, positive
    )
    wide = ((rows, width), f32)
    pair = ((2 * rows, width), bf16)
    core_part, part2 = call(early_kernel, "early", [pair, block], w01, w23, near, far, txts)
    sums, core_part, part2 = call(
        half_kernel, "half", [few, pair, block],
        row_sums, row_core, col_sums, col1, core_part, part2, part2,
    )
    core_part, relayed = swapped(core_part, CORE), moved(part2, relay)
    txt_back, txt_next, token = call(
        text_kernel, "text", [wide, wide, few], w01, w23, near, far, sums
    )
    img_back, first, late = call(
        image_kernel, "image", [wide, block, wide], w01, w23, txts, sums
    )
    (sums,) = call(side_kernel, "side", [few], sums, swapped(sums, 1, "dp"), token, late)
    sums_got = moved(sums, by_sides)
    part_y, first = call(
        across_kernel, "across", [block] * 2, txt_next, core_part, first, sums
    )
    (sums,) = call(side_kernel, "sides", [few], sums, sums_got, part_y, relayed)
    part_y, first = swapped(part_y, Y), moved(first, relay)
    (late,) = call(late_kernel, "late", [block], late, relayed, sums)
    (held,) = call(total_kernel, "total", [few], sums, swapped(sums, CORE), late)
    late = moved(late, other_way)
    (held,) = call(add_kernel, "add", [few], held, moved(held, by_planes))
    (held,) = call(planes_kernel, "planes", [few], held, swapped(held, CORE))
    text_grad, text_token = call(
        grad_kernel, "text_grad", [block, few],
        logit_scale, text, txt_back, core_part, part_y, scalar=True,
    )
    image_grad, image_token = call(
        grad_kernel, "image_grad", [block, few],
        logit_scale, image, img_back, first, late, scalar=True,
    )
    (held,) = call(
        side_kernel, "side", [few], held, moved(held, by_far_planes), text_token, text_token
    )
    total_rows = rows * lax.axis_size("blk") * lax.axis_size("dp")
    loss, scale_grad = pl.pallas_call(
        functools.partial(scalar_kernel, total_rows), name="scalar",
        out_shape=[jax.ShapeDtypeStruct((1,), f32)] * 2,
        in_specs=[SMEM, VMEM, VMEM, VMEM], out_specs=[SMEM] * 2,
        compiler_params=PARAMS,
    )(logit_scale, held, swapped(held, CORE), image_token)
    return (loss, scale_grad, image_grad, text_grad)


def solution(mesh):
    in_specs = (P(("dp", "blk"), None), P(("dp", "blk"), None), P(("dp", "blk")), P())
    out_specs = (P(), P(), P(("dp", "blk"), None), P(("dp", "blk"), None))
    return jax.shard_map(shards, mesh=mesh, in_specs=in_specs, out_specs=out_specs, check_vma=False)
```

```python
import functools
import itertools
import math

import jax
import jax.numpy as jnp
from jax import lax
from jax.experimental import pallas as pl
from jax.experimental.pallas import tpu as pltpu
from jax.sharding import PartitionSpec as P

EPSILON = 1e-06
VMEM = pl.BlockSpec(memory_space=pltpu.VMEM)
SMEM = pl.BlockSpec(memory_space=pltpu.SMEM)
PARAMS = pltpu.CompilerParams(vmem_limit_bytes=24 * 1024 * 1024)
SLOTS = 4
LOW = -1e30
COST = {
    "sides": 10, "total": 10,
    "pick": 5.0,
    "own": 0.25, "first": 12, "second": 8, "third": 1.15, "lse": 0.15, "weight": 1.3,
    "image": 1.1, "text": 1.1, "early": 1.4, "half": 0.3, "across": 0.2, "late": 0.2, "grad": 1.6,
}
NEAR = (0, 1, 3)
X1, X2, X3, Y, CORE = 4, 8, 12, 2, 1


def swapped(value, bits, axis="blk"):
    return lax.ppermute(value, axis, [(i, i ^ bits) for i in range(lax.axis_size(axis))])


def moved(value, step):
    places = itertools.product(range(8), range(2), range(4), range(2), range(2))
    flat = lambda z, lo, x, hi, core: (z % 8 * 2 + lo) * 16 + x * 4 + hi * 2 + core
    pairs = [(flat(*p), flat(*step(*p))) for p in places]
    return lax.ppermute(value, ("dp", "blk"), pairs)


def by_sides(z, lo, x, hi, core):
    return (z, 1 - lo, x, 1 - hi, core) if core == 0 else (z, lo, 3 - x, hi, core)


def relay(z, lo, x, hi, core):
    return (z, lo, x ^ 1 if core == 0 else 3 - x, hi, core)


def other_way(z, lo, x, hi, core):
    return (z, lo, 3 - x if core == 0 else x ^ 1, hi, core)


def by_planes(z, lo, x, hi, core):
    return (z + (1 if (z + core) % 2 == 0 else -1), lo, x, hi, core)


def by_far_planes(z, lo, x, hi, core):
    return (z + (-3 if core == 0 else 3), lo, x, hi, core)


def call(kernel, name, outs, *args, scalar=False):
    specs = [SMEM] * scalar + [VMEM] * (len(args) - scalar)
    moved = sum(a.size * a.dtype.itemsize for a in args)
    moved += sum(math.prod(s) * jnp.dtype(d).itemsize for s, d in outs)
    return pl.pallas_call(
        kernel, out_shape=[jax.ShapeDtypeStruct(s, d) for s, d in outs], in_specs=specs,
        out_specs=[VMEM] * len(outs), name=name,
        cost_estimate=pl.CostEstimate(
            flops=int(COST.get(name, 0.05) * 1.1e9), bytes_accessed=moved, transcendentals=0
        ),
        compiler_params=PARAMS,
    )(*args)


def eye(n):
    return lax.broadcasted_iota(jnp.int32, (n, n), 0) == lax.broadcasted_iota(jnp.int32, (n, n), 1)


def to_row(column, diagonal):
    return jnp.sum(jnp.where(diagonal, column, 0.0), axis=0, keepdims=True)


def to_column(row, diagonal):
    return jnp.sum(jnp.where(diagonal, row, 0.0), axis=1, keepdims=True)


def unit_rows(values):
    wide = values.astype(jnp.float32)
    inverse = lax.rsqrt(jnp.sum(wide * wide, axis=-1, keepdims=True) + EPSILON)
    return wide * inverse, inverse


def hits(positive, diagonal):
    target = to_column(positive[...].astype(jnp.float32), diagonal).astype(jnp.int32)
    return lax.broadcasted_iota(jnp.int32, diagonal.shape, 1) == target


def merged(a, b):
    top = jnp.maximum(a[0], b[0])
    ea, eb = jnp.exp(a[0] - top), jnp.exp(b[0] - top)
    both = ea + eb
    return top + jnp.log(both), (a[1] * ea + b[1] * eb) / both


def into(part, span, value):
    part[0:1, span], part[1:2, span] = merged((part[0:1, span], part[1:2, span]), value)


def stats(scale, imgs, txts, logits, row_part, col_part):
    diagonal = eye(next(iter(txts.values())).shape[0])
    rows = diagonal.shape[0]
    slots, blocks = tuple(imgs), tuple(txts)
    at = lambda k: pl.ds(k * rows, rows)
    row_top, col_top = {}, {}
    for l in blocks:
        for k in slots:
            tile = scale * lax.dot_general(
                imgs[k][...], txts[l][...], (((1,), (1,)), ((), ())),
                preferred_element_type=jnp.float32,
            )
            logits[k, l][...] = tile
            right = jnp.max(tile, axis=1, keepdims=True)
            down = jnp.max(tile, axis=0, keepdims=True)
            row_top[k] = jnp.maximum(row_top[k], right) if k in row_top else right
            col_top[l] = jnp.maximum(col_top[l], down) if l in col_top else down
    none = jnp.zeros((1, rows), jnp.float32)
    col_sum, col_moment = {l: none for l in blocks}, {l: none for l in blocks}
    for k in slots:
        total = jnp.zeros((rows, 1), jnp.float32)
        moment = jnp.zeros((rows, 1), jnp.float32)
        for l in blocks:
            tile = logits[k, l][...]
            e = jnp.exp(tile - row_top[k])
            total += jnp.sum(e, axis=1, keepdims=True)
            moment += jnp.sum(e * tile, axis=1, keepdims=True)
            f = jnp.exp(tile - col_top[l])
            col_sum[l] += jnp.sum(f, axis=0, keepdims=True)
            col_moment[l] += jnp.sum(f * tile, axis=0, keepdims=True)
        total = to_row(total, diagonal)
        top = to_row(row_top[k], diagonal)
        into(row_part, at(k), (top + jnp.log(total), to_row(moment, diagonal) / total))
    for l in blocks:
        into(col_part, at(l), (col_top[l] + jnp.log(col_sum[l]), col_moment[l] / col_sum[l]))


def unit(values):
    return unit_rows(values[...])[0].astype(jnp.bfloat16)


def views(ref, slots, rows):
    return {k: ref.at[pl.ds(n * rows, rows), :] for n, k in enumerate(slots)}


def tiles(ref, slots, blocks, rows):
    return {
        (k, l): ref.at[pl.ds(n * rows, rows), pl.ds(m * rows, rows)]
        for n, k in enumerate(slots) for m, l in enumerate(blocks)
    }


def own_kernel(image, text, img_unit, txt_unit):
    img_unit[...] = unit(image)
    txt_unit[...] = unit(text)


def first_kernel(
    scale, i0, t0, i1, i3, t1, t2, positive, near, txts, logits, row_part, col_part
):
    rows = i0.shape[0]
    imgs, texts = views(near, NEAR, rows), views(txts, (0, 1, 2), rows)
    imgs[0][...] = i0[...]
    texts[0][...] = t0[...]
    imgs[1][...], imgs[3][...] = unit(i1), unit(i3)
    texts[1][...], texts[2][...] = unit(t1), unit(t2)
    for part in (row_part, col_part):
        part[0:1, :] = jnp.full((1, SLOTS * rows), LOW, jnp.float32)
        part[1:4, :] = jnp.zeros((3, SLOTS * rows), jnp.float32)
    scores = tiles(logits, NEAR, (0, 1, 2), rows)
    stats(scale[0], imgs, texts, scores, row_part, col_part)
    matched = jnp.where(hits(positive, eye(rows)), scores[0, 0][...], 0.0)
    row_part[2:3, pl.ds(0, rows)] = jnp.sum(matched, axis=0, keepdims=True)


def core_index():
    return lax.axis_index("blk") % 2


def pick_kernel(i1, i3, before, out):
    core = core_index()

    @pl.when(core == 0)
    def _():
        out[...] = i3[...]

    @pl.when(core != 0)
    def _():
        out[...] = i1[...]


def second_kernel(scale, t3, near, txts_in, row_in, col_in, txts, logits, row_part, col_part):
    rows = t3.shape[0]
    row_part[...] = row_in[...]
    col_part[...] = col_in[...]
    txts[pl.ds(0, 3 * rows), :] = txts_in[...]
    last = txts.at[pl.ds(3 * rows, rows), :]
    last[...] = unit(t3)
    scores = tiles(logits, NEAR, (3,), rows)
    stats(scale[0], views(near, NEAR, rows), {3: last}, scores, row_part, col_part)


def third_kernel(scale, i2, txts, row_in, col_in, far, logits, row_part, col_part):
    rows = i2.shape[0]
    row_part[...] = row_in[...]
    col_part[...] = col_in[...]
    far[...] = unit(i2)
    blocks = range(SLOTS)
    scores = tiles(logits, (2,), blocks, rows)
    stats(scale[0], {2: far}, views(txts, blocks, rows), scores, row_part, col_part)


def joined(mine, other, bits):
    rows = mine.shape[1] // SLOTS
    swap = lambda at: jnp.concatenate(
        [other[at : at + 1, (k ^ bits) * rows : ((k ^ bits) + 1) * rows] for k in range(SLOTS)],
        axis=1,
    )
    value, mean = merged((mine[0:1, :], mine[1:2, :]), (swap(0), swap(1)))
    return value, mean, mine[2:3, :] + swap(2)


def join_kernel(bits, mine, other, out):
    out[0:1, :], out[1:2, :], out[2:3, :] = joined(mine, other, bits)
    out[3:, :] = jnp.zeros((out.shape[0] - 3, out.shape[1]), jnp.float32)


def slot_sum(v):
    rows = v.shape[1] // SLOTS
    at = [jnp.sum(v[:, k * rows : (k + 1) * rows], axis=1, keepdims=True) for k in range(SLOTS)]
    return (at[0] + at[1]) + (at[2] + at[3])


def lse_kernel(row, row1, col, col2, lse, row_sums, col_sums):
    lane = lax.broadcasted_iota(jnp.int32, row_sums.shape, 1)
    sides = ((joined(row, row1, 1), row_sums), (joined(col, col2, 2), col_sums))
    for at, ((value, mean, matched), out) in enumerate(sides):
        lse[at : at + 1, :] = value
        loss, slope = slot_sum(0.5 * value - matched), slot_sum(0.5 * mean - matched)
        out[...] = jnp.where(lane == 0, loss, jnp.where(lane == 1, slope, 0.0))


def weigh(scores, lse, slots, w, hit=None):
    rows = lse.shape[1] // SLOTS
    diagonal = eye(rows)
    at = lambda k: pl.ds(k * rows, rows)
    for k in slots:
        right = to_column(lse[0:1, at(k)], diagonal)
        for l in range(SLOTS):
            tile = scores[k, l][...]
            weight = 0.5 * (jnp.exp(tile - right) + jnp.exp(tile - lse[1:2, at(l)]))
            if k == 0 and l == 0:
                weight = weight - hit.astype(jnp.float32)
            w[k, l][...] = weight.astype(jnp.bfloat16)


def over(w01, w23, near, far, l):
    rows = far.shape[0]
    span = pl.ds(l * rows, rows)
    term = lambda weights, blocks: lax.dot_general(
        weights, blocks, (((0,), (0,)), ((), ())), preferred_element_type=jnp.float32
    )
    one, two = pl.ds(0, rows), pl.ds(rows, rows)
    return (
        term(w01[:, span], near[pl.ds(0, 2 * rows), :])
        + term(w23[one, span], far[...])
        + term(w23[two, span], near[pl.ds(2 * rows, rows), :])
    )


def weight_kernel(first, second, third, lse, positive, w01, w23):
    rows = w01.shape[0] // 2
    scores = tiles(first, NEAR, (0, 1, 2), rows)
    scores.update(tiles(second, NEAR, (3,), rows))
    scores.update(tiles(third, (2,), range(SLOTS), rows))
    hit = hits(positive, eye(rows))
    weigh(scores, lse, (2, 3), tiles(w23, (2, 3), range(SLOTS), rows))
    weigh(scores, lse, (0, 1), tiles(w01, (0, 1), range(SLOTS), rows), hit)


def early_kernel(w01, w23, near, far, txts, core_part, part2):
    rows = far.shape[0]
    back = jnp.dot(w23[pl.ds(0, rows), :], txts[...], preferred_element_type=jnp.float32)
    part2[...] = back.astype(part2.dtype)
    for n, l in enumerate((1, 3)):
        core_part[pl.ds(n * rows, rows), :] = over(w01, w23, near, far, l).astype(core_part.dtype)


def image_kernel(w01, w23, txts, before, img_back, first, late):
    rows = img_back.shape[0]
    back = lambda w, n: jnp.dot(
        w[pl.ds(n * rows, rows), :], txts[...], preferred_element_type=jnp.float32
    )
    zero = core_index() == 0
    one, three = back(w01, 1), back(w23, 1)
    first[...] = jnp.where(zero, one, three).astype(first.dtype)
    late[...] = jnp.where(zero, three, one)
    img_back[...] = back(w01, 0)


def half_kernel(row, row_core, col, col1, core_in, part2_in, before, sums, core_part, part2):
    sums[...] = jnp.where(core_index() == 0, row[...] + row_core[...], col[...] + col1[...])
    core_part[...] = core_in[...]
    part2[...] = part2_in[...]


def text_kernel(w01, w23, near, far, before, txt_back, txt_next, token):
    token[...] = jnp.zeros(token.shape, jnp.float32)
    for out, l in ((txt_back, 0), (txt_next, 2)):
        out[...] = over(w01, w23, near, far, l)


def across_kernel(txt_next, core_part, first_in, before, part_y, first):
    rows = part_y.shape[0]
    first[...] = first_in[...]
    total = txt_next[...] + core_part[pl.ds(rows, rows), :].astype(jnp.float32)
    part_y[...] = total.astype(part_y.dtype)


def late_kernel(late, relayed, before, out):
    out[...] = (late[...] + relayed[...].astype(jnp.float32)).astype(out.dtype)


def side_kernel(a, b, before, before_too, out):
    out[...] = a[...] + b[...]


def add_kernel(a, b, out):
    out[...] = a[...] + b[...]


def lane_from_z(shape):
    lane = lax.broadcasted_iota(jnp.int32, shape, 1)
    return (lane - lax.axis_index("dp") // 2 + 8) % 8, lane < 8


def total_kernel(mine, other, before, held):
    sums = mine[0:1, :] + other[0:1, :]
    line = lax.broadcasted_iota(jnp.int32, held.shape, 0)
    value = jnp.where(line == 0, sums[:, 0:1], jnp.where(line == 1, sums[:, 1:2], 0.0))
    ahead, inside = lane_from_z(held.shape)
    held[...] = jnp.where(inside & (ahead == 0), value, 0.0)


def union(held, other, both):
    ahead, _ = lane_from_z(held.shape)
    twice = functools.reduce(jnp.logical_or, [ahead == n for n in both])
    return jnp.where(twice, held[...], held[...] + other[...])


def planes_kernel(held, other, out):
    out[...] = union(held, other, (0,))


def scalar_kernel(total_rows, scale, held, other, loss, scale_grad):
    sums = jnp.sum(union(held, other, (0, 1, 4, 7)), axis=1, keepdims=True)
    loss[0] = sums[0, 0] / total_rows
    scale_grad[0] = sums[1, 0] / (total_rows * scale[0])


def grad_kernel(scale, image, text, img_back, txt_back, core_part, first, late, py, image_grad, text_grad, token):
    token[...] = jnp.zeros(token.shape, jnp.float32)
    for values, parts, out in (
        (image, (img_back, first, late), image_grad), (text, (txt_back, core_part, py), text_grad),
    ):
        direction, inverse = unit_rows(values[...])
        incoming = scale[0] * sum(
            part[pl.ds(0, direction.shape[0]), :].astype(jnp.float32) for part in parts
        )
        along = jnp.sum(direction * incoming, axis=-1, keepdims=True)
        out[...] = ((incoming - direction * along) * inverse).astype(out.dtype)


def shards(image, text, positive, logit_scale):
    rows, width = image.shape
    group = SLOTS * rows
    f32, bf16 = jnp.float32, jnp.bfloat16
    block, parts = ((rows, width), bf16), ((SLOTS, group), f32)
    positive = positive.reshape(1, rows)

    i1, i3 = swapped(image, X1), swapped(image, X3)
    t1, t2 = swapped(text, CORE), swapped(text, Y)
    own_img, own_txt = call(own_kernel, "own", [block] * 2, image, text)
    (on,) = call(pick_kernel, "pick", [block], i1, i3, own_img)
    i2 = moved(on, relay)
    t3 = swapped(t2, CORE)
    three = group - rows
    near, txts, first, row_part, col_part = call(
        first_kernel, "first", [((three, width), bf16)] * 2 + [((three, three), f32), parts, parts],
        logit_scale, own_img, own_txt, i1, i3, t1, t2, positive, scalar=True,
    )
    txts, second, row_part, col_part = call(
        second_kernel, "second", [((group, width), bf16), ((three, rows), f32), parts, parts],
        logit_scale, t3, near, txts, row_part, col_part, scalar=True,
    )
    few = ((8, 128), f32)
    far, third, row_part, col_part = call(
        third_kernel, "third", [block, ((rows, group), f32), parts, parts],
        logit_scale, i2, txts, row_part, col_part, scalar=True,
    )
    (col_part,) = call(
        functools.partial(join_kernel, 1), "join", [((2 * SLOTS, group), f32)],
        col_part, swapped(col_part, CORE),
    )
    col_y = swapped(col_part, Y)
    (row_part,) = call(
        functools.partial(join_kernel, 3), "join", [parts], row_part, swapped(row_part, X3)
    )
    lse, row_sums, col_sums = call(
        lse_kernel, "lse", [((2, group), f32), few, few],
        row_part, swapped(row_part, X1), col_part, col_y,
    )
    row_core, col1 = swapped(row_sums, CORE), swapped(col_sums, X1)
    heavy = ((2 * rows, group), bf16)
    w01, w23 = call(
        weight_kernel, "weight", [heavy, heavy], first, second, third, lse, positive
    )
    wide = ((rows, width), f32)
    pair = ((2 * rows, width), bf16)
    core_part, part2 = call(early_kernel, "early", [pair, block], w01, w23, near, far, txts)
    sums, core_part, part2 = call(
        half_kernel, "half", [few, pair, block],
        row_sums, row_core, col_sums, col1, core_part, part2, part2,
    )
    core_part, relayed = swapped(core_part, CORE), moved(part2, relay)
    txt_back, txt_next, token = call(
        text_kernel, "text", [wide, wide, few], w01, w23, near, far, sums
    )
    img_back, first, late = call(
        image_kernel, "image", [wide, block, wide], w01, w23, txts, sums
    )
    (sums,) = call(side_kernel, "side", [few], sums, swapped(sums, 1, "dp"), token, late)
    sums_got = moved(sums, by_sides)
    part_y, first = call(
        across_kernel, "across", [block] * 2, txt_next, core_part, first, sums
    )
    (sums,) = call(side_kernel, "sides", [few], sums, sums_got, part_y, relayed)
    part_y, first = swapped(part_y, Y), moved(first, relay)
    (late,) = call(late_kernel, "late", [block], late, relayed, sums)
    (held,) = call(total_kernel, "total", [few], sums, swapped(sums, CORE), late)
    late = moved(late, other_way)
    (held,) = call(add_kernel, "add", [few], held, moved(held, by_planes))
    (held,) = call(planes_kernel, "planes", [few], held, swapped(held, CORE))
    image_grad, text_grad, token = call(
        grad_kernel, "grad", [block] * 2 + [few],
        logit_scale, image, text, img_back, txt_back, core_part, first, late, part_y, scalar=True,
    )
    (held,) = call(
        side_kernel, "side", [few], held, moved(held, by_far_planes), token, token
    )
    total_rows = rows * lax.axis_size("blk") * lax.axis_size("dp")
    loss, scale_grad = pl.pallas_call(
        functools.partial(scalar_kernel, total_rows), name="scalar",
        out_shape=[jax.ShapeDtypeStruct((1,), f32)] * 2,
        in_specs=[SMEM, VMEM, VMEM], out_specs=[SMEM] * 2,
        compiler_params=PARAMS,
    )(logit_scale, held, swapped(held, CORE))
    return (loss, scale_grad, image_grad, text_grad)


def solution(mesh):
    in_specs = (P(("dp", "blk"), None), P(("dp", "blk"), None), P(("dp", "blk")), P())
    out_specs = (P(), P(), P(("dp", "blk"), None), P(("dp", "blk"), None))
    return jax.shard_map(shards, mesh=mesh, in_specs=in_specs, out_specs=out_specs, check_vma=False)
```
